32 devices in a mesh: dp: 2 (over core), ctx: 8 (over z, x), head: 2 (over y).
Axes of the slice: x: 2, y: 2, z: 4, core: 2. Of those that a mesh axis runs over, the one named last changes fastest.
Arguments:
- query: bfloat16 [2, 8, 2, 512, 512], P('dp', 'ctx', 'head'), may hold values from -120 to 120
- key: bfloat16 [2, 1024, 4096], P('dp', 'ctx', 'head'), may hold values from -8 to 8
- value: bfloat16 [2, 1024, 4096], P('dp', 'ctx', 'head'), may hold values from -6 to 6
- grad_out: bfloat16 [2, 8, 2, 512, 512], P('dp', 'ctx', 'head'), may hold values from -6 to 6
- chosen: int32 [2, 2, 32, 3], P('dp', None, 'head'), may hold values from 0 to 1, as said below
- placed: int32 [2], replicated, may hold values from 0 to 1, each once
- sink: float32 [32], P('head'), may hold values from -2 to 6
Outputs:
- attended: bfloat16 [2, 8, 2, 512, 512], P('dp', 'ctx', 'head')
- grad_query: bfloat16 [2, 8, 2, 512, 512], P('dp', 'ctx', 'head')
- grad_key: bfloat16 [2, 1024, 4096], P('dp', 'ctx', 'head')
- grad_value: bfloat16 [2, 1024, 4096], P('dp', 'ctx', 'head')
- grad_sink: float32 [32], replicated
The draws below stay inside these ranges and needn't reach their ends.
Inputs may be any that keep to these rules, and one draw needn't show every extreme that they name: `chosen`: for each sequence, block b and head, the first min(b, 3) entries are distinct blocks before b; the remaining entries are blocks from b to 1. `placed`: every block is held by exactly one slot.
All inputs are finite; a program needn't handle non-finite values.
Results may differ from the reference program's by a relative error of at most 0.025.
Values may be sent and summed in bfloat16 or wider, within the bound.
A program may use at most 64 MiB of HBM per device.

```python
import math
import jax
import jax.numpy as jnp
from jax import lax

HEADS = 32
DH = 128
BLOCK = 512
SPB = 4
TOPK = 3
HPD = 4
NB = 2
SEQ = 1024
BATCH = 2
N_CTX = 8
N_HEAD = 2


def joint_draw(key):
    shape = (BATCH, SEQ, HEADS, DH)
    key_raw = jax.random.normal(jax.random.fold_in(key, 101), shape, jnp.float32)
    query_raw = jax.random.normal(jax.random.fold_in(key, 202), shape, jnp.float32)
    return (query_raw, key_raw)


def draw_query(key, part):
    query_raw, key_raw = joint_draw(key)
    groups = HEADS // (SPB * HPD)
    shaped = query_raw.reshape(BATCH, NB, BLOCK, groups, SPB, HPD, DH)
    moved = jnp.transpose(shaped, (0, 1, 4, 3, 2, 5, 6))
    return moved.reshape(BATCH, NB * SPB, groups, BLOCK, HPD * DH).astype(jnp.bfloat16)


def draw_key(key, part):
    query_raw, key_raw = joint_draw(key)
    return key_raw.reshape(BATCH, SEQ, HEADS * DH).astype(jnp.bfloat16)


def draw_chosen(key, part):
    raw = jax.random.randint(key, (BATCH, NB, HEADS, NB), 0, 1 << 20)
    cand = jnp.arange(NB, dtype=jnp.int32)
    own = jnp.arange(NB, dtype=jnp.int32)[None, :, None, None]
    score = jnp.where(cand < own, raw * NB + cand + 1, -1 - cand)
    count = min(TOPK, NB)
    best, where_at = lax.top_k(score, count)
    if count < TOPK:
        pad_shape = (BATCH, NB, HEADS, TOPK - count)
        best = jnp.concatenate([best, jnp.full(pad_shape, -1, best.dtype)], axis=-1)
        where_at = jnp.concatenate([where_at, jnp.zeros(pad_shape, where_at.dtype)], axis=-1)
    shape = (BATCH, NB, HEADS, TOPK)
    spread = jax.random.randint(jax.random.fold_in(key, 7), shape, 0, 1 << 20)
    later = own + spread % (NB - own)
    picked = jnp.where(best > 0, where_at.astype(jnp.int32), later)
    entry = jnp.arange(TOPK, dtype=jnp.int32)[None, None, None, :]
    picked = jnp.where((own == 0) & (entry == 0), NB - 1, picked)
    return picked.astype(jnp.int32)


def shard_levels(rng, dims, pieces, low, high):
    loudness, own = 1.0, jax.random.fold_in(rng, 6)
    for axis_at, blocks in pieces:
        heights = jnp.exp(jax.random.uniform(jax.random.fold_in(own, axis_at), (blocks,), jnp.float32, low / len(pieces), high / len(pieces)))
        loudness = loudness * jnp.repeat(heights, dims[axis_at] // blocks).reshape([-1 if axis == axis_at else 1 for axis in range(len(dims))])
    return loudness


def centred(stream_key, extent, scale, reach, cuts=(), kind=jnp.bfloat16):
    result = scale * jax.random.normal(stream_key, extent, jnp.float32)
    if cuts:
        result = result * shard_levels(stream_key, extent, cuts, -0.22, 0.18)
    return jnp.clip(result, -reach, reach).astype(kind)


def setup_inputs(seed: int = 0) -> dict:
    arg_keys = jax.random.split(jax.random.key(seed), 8)
    return {
        "query": draw_query(jax.random.fold_in(arg_keys[7], 71), 0),
        "key": draw_key(jax.random.fold_in(arg_keys[7], 71), 0),
        "value": centred(arg_keys[2], (BATCH, SEQ, HEADS * DH), 1.0, 6.0, ((0, 2), (1, 8), (2, 2))),
        "grad_out": centred(arg_keys[3], (BATCH, N_CTX, N_HEAD, BLOCK, HPD * DH), 1.0, 6.0, ((0, 2), (1, 8), (2, 2))),
        "chosen": draw_chosen(jax.random.fold_in(arg_keys[7], 71), 0),
        "placed": jax.random.permutation(arg_keys[5], NB).astype(jnp.int32),
        "sink": jnp.clip(-2.0 + 8.0 * jax.random.uniform(arg_keys[6], (HEADS,), jnp.float32) ** shard_levels(arg_keys[6], (HEADS,), ((0, 2),), -0.2, 0.2), -2.0, 6.0),
    }


def inner_rows(left, right):
    return lax.dot_general(left, right, (((1,), (1,)), ((), ())), preferred_element_type=jnp.float32)

def outer_rows(left, right):
    return lax.dot_general(left, right, (((0,), (0,)), ((), ())), preferred_element_type=jnp.float32)

def attend_block(query_rows, grad_rows, tiles, usable, sink_logit):
    rows, width = query_rows.shape
    scale = 1.0 / math.sqrt(width)
    keys = tiles[:, :, :width].reshape(-1, width)
    vals = tiles[:, :, width:].reshape(-1, width)
    scores = inner_rows(query_rows, keys) * scale
    cols = tiles.shape[0] * rows
    tile_of = jnp.arange(cols) // rows
    offset = jnp.arange(cols) % rows
    own_ok = offset[None, :] <= jnp.arange(rows)[:, None]
    allowed = jnp.where(tile_of[None, :] == 0, own_ok, usable[tile_of][None, :])
    masked = jnp.where(allowed, scores, -jnp.inf)
    top = jnp.maximum(lax.optimization_barrier(jnp.max(masked, axis=1)), sink_logit)
    expo = jnp.exp(masked - top[:, None])
    sink_part = jnp.exp(sink_logit - top)
    total = sink_part + lax.optimization_barrier(jnp.sum(expo, axis=1))
    prob = expo / total[:, None]
    weights = prob.astype(jnp.bfloat16)
    attended = jnp.dot(weights, vals, preferred_element_type=jnp.float32).astype(jnp.bfloat16)
    stored = lax.optimization_barrier(attended)
    delta = lax.optimization_barrier(jnp.sum(grad_rows.astype(jnp.float32) * stored.astype(jnp.float32), axis=1))
    dprob = inner_rows(grad_rows, vals)
    dscore = (prob * (dprob - delta[:, None]) * scale).astype(jnp.bfloat16)
    grad_query = jnp.dot(dscore, keys, preferred_element_type=jnp.float32).astype(jnp.bfloat16)
    grad_keys = outer_rows(dscore, query_rows).astype(jnp.bfloat16)
    grad_vals = outer_rows(weights, grad_rows).astype(jnp.bfloat16)
    tiles_grad = jnp.concatenate([grad_keys, grad_vals], axis=1).reshape(tiles.shape)
    sink_grad = -jnp.sum(sink_part / total * delta)
    return (attended, grad_query, tiles_grad, sink_grad)

def reference(query, key, value, grad_out, chosen, placed, sink):
    groups = HEADS // (SPB * HPD)

    def to_heads(arr):
        shaped = arr.reshape(BATCH, NB, SPB, groups, BLOCK, HPD, DH)
        return jnp.transpose(shaped, (0, 3, 2, 5, 1, 4, 6)).reshape(BATCH * HEADS, NB, BLOCK, DH)

    def from_heads(arr):
        shaped = arr.reshape(BATCH, groups, SPB, HPD, NB, BLOCK, DH)
        return jnp.transpose(shaped, (0, 4, 2, 1, 5, 3, 6)).reshape(BATCH, NB * SPB, groups, BLOCK, HPD * DH)

    def token_heads(arr):
        shaped = arr.reshape(BATCH, NB, BLOCK, HEADS, DH)
        return jnp.transpose(shaped, (0, 3, 1, 2, 4)).reshape(BATCH * HEADS, NB, BLOCK, DH)
    query_heads = to_heads(query)
    grad_heads = to_heads(grad_out)
    paired = jnp.concatenate([token_heads(key), token_heads(value)], axis=-1)
    picks_all = jnp.transpose(chosen, (0, 2, 1, 3)).reshape(BATCH * HEADS, NB, TOPK)
    sink_all = jnp.tile(sink, BATCH)
    slot_of = jnp.zeros((NB,), jnp.int32).at[placed].set(jnp.arange(NB, dtype=jnp.int32))

    def per_pair(item):
        q_all, g_all, kv_all, pick_all, sink_logit = item

        def step(acc, slot):
            seq_block = placed[slot]
            cand = pick_all[seq_block]
            good = cand < seq_block
            mapped = jnp.where(good, slot_of[cand], slot)
            index = jnp.concatenate([slot[None], mapped]).astype(jnp.int32)
            tiles = kv_all[index]
            usable = jnp.concatenate([jnp.ones((1,), bool), good])
            att, gq, tg, sg = attend_block(q_all[slot], g_all[slot], tiles, usable, sink_logit)
            acc = acc.at[index].add(tg.astype(jnp.float32))
            return (acc, (att, gq, sg))
        start = jnp.zeros(kv_all.shape, jnp.float32)
        acc, outs = lax.scan(step, start, jnp.arange(NB, dtype=jnp.int32))
        return (outs[0], outs[1], acc.astype(jnp.bfloat16), jnp.sum(outs[2]))
    att, gq, kvg, sgs = lax.map(per_pair, (query_heads, grad_heads, paired, picks_all, sink_all))
    attended = from_heads(att)
    grad_query = from_heads(gq)

    def back_tokens(arr):
        shaped = arr.reshape(BATCH, HEADS, SEQ, DH)
        return jnp.transpose(shaped, (0, 2, 1, 3)).reshape(BATCH, SEQ, HEADS * DH)
    grad_key = back_tokens(kvg[..., :DH])
    grad_value = back_tokens(kvg[..., DH:])
    grad_sink = lax.optimization_barrier(jnp.sum(sgs.reshape(BATCH, HEADS), axis=0))
    return (attended, grad_query, grad_key, grad_value, grad_sink)
```

```python
import functools
import math

import jax
import jax.numpy as jnp
from jax import lax
from jax.experimental import pallas as pl
from jax.experimental.pallas import tpu as pltpu
from jax.sharding import PartitionSpec as P

HEADS = 32
DH = 128


def inner_rows(left, right):
    return lax.dot_general(
        left, right, (((1,), (1,)), ((), ())), preferred_element_type=jnp.float32
    )


def outer_rows(left, right):
    return lax.dot_general(
        left, right, (((0,), (0,)), ((), ())), preferred_element_type=jnp.float32
    )


def attend_block(query_rows, grad_rows, tiles, usable, sink_logit):
    rows, width = query_rows.shape
    scale = 1.0 / math.sqrt(width)
    keys = tiles[:, :, :width].reshape(-1, width)
    vals = tiles[:, :, width:].reshape(-1, width)
    scores = inner_rows(query_rows, keys) * scale
    cols = tiles.shape[0] * rows
    tile_of = jnp.arange(cols) // rows
    offset = jnp.arange(cols) % rows
    own_ok = offset[None, :] <= jnp.arange(rows)[:, None]
    allowed = jnp.where(tile_of[None, :] == 0, own_ok, usable[tile_of][None, :])
    masked = jnp.where(allowed, scores, -jnp.inf)
    top = jnp.maximum(jnp.max(masked, axis=1), sink_logit)
    expo = jnp.exp(masked - top[:, None])
    sink_part = jnp.exp(sink_logit - top)
    total = sink_part + jnp.sum(expo, axis=1)
    prob = expo / total[:, None]
    weights = prob.astype(jnp.bfloat16)
    attended = jnp.dot(weights, vals, preferred_element_type=jnp.float32).astype(jnp.bfloat16)
    stored = lax.optimization_barrier(attended)
    delta = jnp.sum(grad_rows.astype(jnp.float32) * stored.astype(jnp.float32), axis=1)
    dprob = inner_rows(grad_rows, vals)
    dscore = (prob * (dprob - delta[:, None]) * scale).astype(jnp.bfloat16)
    grad_query = jnp.dot(dscore, keys, preferred_element_type=jnp.float32).astype(jnp.bfloat16)
    grad_keys = outer_rows(dscore, query_rows).astype(jnp.bfloat16)
    grad_vals = outer_rows(weights, grad_rows).astype(jnp.bfloat16)
    tiles_grad = jnp.concatenate([grad_keys, grad_vals], axis=1).reshape(tiles.shape)
    sink_grad = -jnp.sum(sink_part / total * delta)
    return (attended, grad_query, tiles_grad, sink_grad)


def general_body(query, key, value, grad_out, chosen, placed, sink):
    seqs = query.shape[0]
    block = query.shape[3]
    width = DH
    hpd = query.shape[4] // width
    unit = key.shape[1]
    parts_per = block // unit
    n_ctx = lax.axis_size("ctx")
    nblk = n_ctx // parts_per
    place = lax.axis_index("ctx")
    slot = place // parts_per
    position = place % parts_per
    slots = jnp.arange(nblk, dtype=jnp.int32)
    seq_block = jnp.sum(jnp.where(slots == slot, placed, 0))
    slot_of = jnp.sum(jnp.where(placed[None, :] == slots[:, None], slots[None, :], 0), axis=1)
    mine = lax.dynamic_slice_in_dim(chosen, seq_block, 1, 1)[:, 0]
    mine = lax.dynamic_slice_in_dim(mine, position * hpd, hpd, 1)
    usable_pick = mine < seq_block
    mapped = jnp.sum(jnp.where(mine[..., None] == slots, slot_of, 0), axis=-1)
    mapped = jnp.where(usable_pick, mapped, slot)
    lead = jnp.broadcast_to(slot, mine.shape[:2] + (1,))
    picks = jnp.concatenate([lead, mapped], axis=-1)
    kinds = picks.shape[-1]
    usable = jnp.concatenate([jnp.ones(mine.shape[:2] + (1,), bool), usable_pick], axis=-1)
    sink_mine = lax.dynamic_slice_in_dim(sink, position * hpd, hpd)
    paired = jnp.concatenate(
        [
            key.reshape(seqs, unit, parts_per, hpd, width),
            value.reshape(seqs, unit, parts_per, hpd, width),
        ],
        axis=-1,
    )
    paired = jnp.transpose(paired, (2, 0, 3, 1, 4))
    items = seqs * hpd
    frag = unit * 2 * width // n_ctx
    seq_ix = jnp.arange(seqs, dtype=jnp.int32)[None, :, None, None, None]
    head_ix = jnp.arange(hpd, dtype=jnp.int32)[None, None, :, None, None]
    spread = jnp.transpose(paired.reshape(parts_per, seqs, hpd, n_ctx, frag), (3, 0, 1, 2, 4))
    held = lax.all_to_all(spread, "ctx", split_axis=0, concat_axis=0, tiled=True)
    held = jnp.transpose(held, (2, 3, 0, 1, 4)).reshape(seqs, hpd, n_ctx * parts_per, frag)
    match_block = placed[:, None] == slots[None, :]
    chosen_all = jnp.sum(jnp.where(match_block[None, :, :, None, None], chosen[:, None], 0), axis=2)
    before = chosen_all < placed[None, :, None, None]
    mapped_all = jnp.sum(jnp.where(chosen_all[..., None] == slots, slot_of, 0), axis=-1)
    own_slot = slots[None, :, None, None]
    mapped_all = jnp.where(before, mapped_all, own_slot)
    lead_all = jnp.broadcast_to(own_slot, mapped_all.shape[:3] + (1,))
    picks_all = jnp.concatenate([lead_all, mapped_all], axis=-1)
    picks_all = jnp.transpose(
        picks_all.reshape(seqs, nblk, parts_per, hpd, kinds), (1, 2, 0, 3, 4)
    ).reshape(n_ctx, seqs, hpd, kinds)
    dest_group = (jnp.arange(n_ctx, dtype=jnp.int32) % parts_per)[:, None, None, None, None]
    part_ids = jnp.arange(parts_per, dtype=jnp.int32)[None, None, None, None, :]
    route = (picks_all[..., None] * parts_per + part_ids) * parts_per + dest_group
    outgoing = held[seq_ix, head_ix, route]
    fetched = lax.all_to_all(outgoing, "ctx", split_axis=0, concat_axis=0, tiled=True)
    tiles_items = jnp.transpose(fetched, (1, 2, 3, 4, 0, 5)).reshape(
        items, kinds, parts_per * unit, 2 * width
    )
    query_heads = jnp.transpose(query.reshape(seqs, block, hpd, width), (0, 2, 1, 3)).reshape(
        items, block, width
    )
    grad_heads = jnp.transpose(grad_out.reshape(seqs, block, hpd, width), (0, 2, 1, 3)).reshape(
        items, block, width
    )
    sink_items = jnp.tile(sink_mine, seqs)

    def per_head(item):
        q_rows, g_rows, tiles, use_row, sink_logit = item
        return attend_block(q_rows, g_rows, tiles, use_row, sink_logit)

    atts, grads_q, tiles_grad, sink_grads = lax.map(
        per_head, (query_heads, grad_heads, tiles_items, usable.reshape(items, -1), sink_items)
    )
    attended = jnp.transpose(atts.reshape(seqs, hpd, block, width), (0, 2, 1, 3)).reshape(
        seqs, 1, 1, block, hpd * width
    )
    grad_query = jnp.transpose(grads_q.reshape(seqs, hpd, block, width), (0, 2, 1, 3)).reshape(
        seqs, 1, 1, block, hpd * width
    )
    shards = tiles_grad.reshape(seqs, hpd, kinds, parts_per, n_ctx, frag)
    sendback = jnp.transpose(shards, (4, 0, 1, 2, 3, 5))
    landed = lax.all_to_all(sendback, "ctx", split_axis=0, concat_axis=0, tiled=True)
    pooled = (
        jnp.zeros((seqs, hpd, n_ctx * parts_per, frag), jnp.float32)
        .at[seq_ix, head_ix, route]
        .add(landed.astype(jnp.float32))
    )
    pooled = jnp.transpose(pooled.reshape(seqs, hpd, n_ctx, parts_per, frag), (2, 3, 0, 1, 4))
    homed = lax.all_to_all(
        pooled.astype(jnp.bfloat16), "ctx", split_axis=0, concat_axis=0, tiled=True
    ).astype(pooled.dtype)
    totals = jnp.transpose(homed, (1, 2, 3, 0, 4)).reshape(parts_per, seqs, hpd, unit, 2 * width)
    totals = jnp.transpose(totals, (1, 3, 0, 2, 4))
    grad_key = totals[..., :width].reshape(seqs, unit, parts_per * hpd * width).astype(jnp.bfloat16)
    grad_value = (
        totals[..., width:].reshape(seqs, unit, parts_per * hpd * width).astype(jnp.bfloat16)
    )
    sink_local = jnp.sum(sink_grads.reshape(seqs, hpd), axis=0)
    start = lax.axis_index("head") * (parts_per * hpd) + position * hpd
    spread_sink = lax.dynamic_update_slice(jnp.zeros((HEADS,), jnp.float32), sink_local, (start,))
    grad_sink = lax.psum(spread_sink, ("dp", "ctx", "head"))
    return (attended, grad_query, grad_key, grad_value, grad_sink)


MESH = pl.DeviceIdType.MESH
ROWS = 256


def two_block_kernel(
    first, parts, hpd, unit,
    q_ref, g_ref, k_ref, v_ref, chosen_ref, sink_ref,
    att_ref, gq_ref, gk_ref, gv_ref, gs_ref,
    keys, vals, key_part, val_part, key_home, val_home, key_sum, val_sum,
    sink_part, sink_ctx, sink_peer,
    in_send, in_recv, out_send, out_recv, sink_send, sink_recv, peer_send, peer_recv,
):
    width = DH
    block = parts * unit
    scale = 1.0 / math.sqrt(width)
    me = lax.axis_index("ctx")
    slot = me // parts
    pos = me % parts
    other = 1 - slot
    is_first = slot == first
    n_ctx = 2 * parts
    mates = [slot * parts + (pos + d) % parts for d in range(1, parts)]
    across = [other * parts + (pos + d) % parts for d in range(parts)]
    peers = [ax for ax in ("head", "dp") if lax.axis_size(ax) > 1]

    barrier = pltpu.get_barrier_semaphore()
    for target in mates + across:
        pl.semaphore_signal(barrier, inc=1, device_id={"ctx": target}, device_id_type=MESH)
    for ax in peers:
        pl.semaphore_signal(barrier, inc=1, device_id={ax: 1 - lax.axis_index(ax)}, device_id_type=MESH)
    pl.semaphore_wait(barrier, n_ctx - 1 + len(peers))

    def cols(at):
        return pl.ds(pl.multiple_of(at * width, width), width)

    def fetch(h, target, source, which):
        src = (k_ref, v_ref)[which]
        dst = (keys, vals)[which]
        return pltpu.make_async_remote_copy(
            src_ref=src.at[:, cols((target % parts) * hpd + h)],
            dst_ref=dst.at[h, source],
            send_sem=in_send.at[which, h, target],
            recv_sem=in_recv.at[which, h, source],
            device_id={"ctx": target},
            device_id_type=MESH,
        )

    def give(h, target, source, which):
        src = (key_part, val_part)[which]
        dst = (key_home, val_home)[which]
        return pltpu.make_async_remote_copy(
            src_ref=src.at[h, target],
            dst_ref=dst.at[h, source],
            send_sem=out_send.at[which, h, target],
            recv_sem=out_recv.at[which, h, source],
            device_id={"ctx": target},
            device_id_type=MESH,
        )

    def each(h, targets, make, act):
        for target in targets:
            for which in range(2):
                if act == "start":
                    make(h, target, me, which).start()
                elif act == "sent":
                    make(h, target, me, which).wait_send()
                else:
                    make(h, me, target, which).wait_recv()

    def send_head(h, carry):
        @pl.when(is_first)
        def _():
            each(h, across, fetch, "start")
        each(h, mates, fetch, "start")
        keys[h, me] = k_ref[:, cols(pos * hpd + h)]
        vals[h, me] = v_ref[:, cols(pos * hpd + h)]
        return carry

    lax.fori_loop(0, hpd, send_head, 0)

    lane = lax.broadcasted_iota(jnp.int32, (8, width), 1)
    top_row = lax.broadcasted_iota(jnp.int32, (8, width), 0) == 0
    sink_part[...] = jnp.zeros((8, width), jnp.float32)

    def attend(h, with_other):
        local_head = pos * hpd + h
        k_own = keys[h, pl.ds(slot * parts, parts)].reshape(block, width)
        v_own = vals[h, pl.ds(slot * parts, parts)].reshape(block, width)
        sink_logit = sink_ref[local_head]
        segs = [(k_own, v_own, 0)]
        if with_other:
            k_oth = keys[h, pl.ds(other * parts, parts)].reshape(block, width)
            v_oth = vals[h, pl.ds(other * parts, parts)].reshape(block, width)
            segs.append((k_oth, v_oth, 1))
            sees = chosen_ref[0, 1, local_head, 0] < 1
            for entry in range(1, chosen_ref.shape[3]):
                sees = jnp.logical_or(sees, chosen_ref[0, 1, local_head, entry] < 1)
            hide = jnp.where(sees, 0.0, -jnp.inf).astype(jnp.float32)
        sink_total = jnp.zeros((1, 1), jnp.float32)
        for r in range(block // ROWS):
            rows = pl.ds(r * ROWS, ROWS)
            q = q_ref[rows, cols(h)]
            g = g_ref[rows, cols(h)]
            used = []
            top = jnp.full((ROWS, 1), sink_logit, jnp.float32)
            for k_all, v_all, kind in segs:
                n = (r + 1) * ROWS if kind == 0 else block
                k, v = k_all[:n], v_all[:n]
                s = inner_rows(q, k) * scale
                if kind == 0:
                    at_row = lax.broadcasted_iota(jnp.int32, (ROWS, n), 0) + r * ROWS
                    at_col = lax.broadcasted_iota(jnp.int32, (ROWS, n), 1)
                    s = jnp.where(at_col <= at_row, s, -jnp.inf)
                else:
                    s = s + hide
                top = jnp.maximum(top, jnp.max(s, axis=1, keepdims=True))
                used.append((k, v, s, kind, n))
            sink_exp = jnp.exp(sink_logit - top)
            total = sink_exp
            expos = []
            for k, v, s, kind, n in used:
                e = jnp.exp(s - top)
                total = total + jnp.sum(e, axis=1, keepdims=True)
                expos.append(e)
            inv = 1.0 / total
            out = jnp.zeros((ROWS, width), jnp.float32)
            probs, weights = [], []
            for (k, v, s, kind, n), e in zip(used, expos):
                p = e * inv
                w = p.astype(jnp.bfloat16)
                out = out + jnp.dot(w, v, preferred_element_type=jnp.float32)
                probs.append(p)
                weights.append(w)
            out = out.astype(jnp.bfloat16)
            att_ref[rows, cols(h)] = out
            delta = jnp.sum(g.astype(jnp.float32) * out.astype(jnp.float32), axis=1, keepdims=True)
            sink_total = sink_total - jnp.sum(sink_exp * inv * delta, axis=0, keepdims=True)
            gq = jnp.zeros((ROWS, width), jnp.float32)
            for (k, v, s, kind, n), p, w in zip(used, probs, weights):
                dprob = inner_rows(g, v)
                ds = (p * (dprob - delta) * scale).astype(jnp.bfloat16)
                gq = gq + jnp.dot(ds, k, preferred_element_type=jnp.float32)
                dk = outer_rows(ds, q)
                dv = outer_rows(w, g)
                if r == 0:
                    key_sum[kind, :n] = dk
                    val_sum[kind, :n] = dv
                    if n < block:
                        key_sum[kind, n:] = jnp.zeros((block - n, width), jnp.float32)
                        val_sum[kind, n:] = jnp.zeros((block - n, width), jnp.float32)
                else:
                    key_sum[kind, :n] += dk
                    val_sum[kind, :n] += dv
            gq_ref[rows, cols(h)] = gq.astype(jnp.bfloat16)
        mine = jnp.logical_and(lane == lax.axis_index("head") * (parts * hpd) + local_head, top_row)
        sink_part[...] += jnp.where(mine, sink_total, 0.0)
        for kind, place in ((0, slot), (1, other))[: 2 if with_other else 1]:
            at = pl.ds(place * parts, parts)
            key_part[h, at] = key_sum[kind].astype(jnp.bfloat16).reshape(parts, unit, width)
            val_part[h, at] = val_sum[kind].astype(jnp.bfloat16).reshape(parts, unit, width)

    def head_step(h, carry):
        each(h, mates, fetch, "arrived")

        @pl.when(is_first)
        def _():
            attend(h, False)

        @pl.when(jnp.logical_not(is_first))
        def _():
            each(h, across, fetch, "arrived")
            attend(h, True)
            each(h, across, give, "start")

        each(h, mates, give, "start")
        key_home[h, me] = key_part[h, me]
        val_home[h, me] = val_part[h, me]
        return carry

    lax.fori_loop(0, hpd, head_step, 0)

    def share(target, source):
        return pltpu.make_async_remote_copy(
            src_ref=sink_part,
            dst_ref=sink_ctx.at[source],
            send_sem=sink_send.at[target],
            recv_sem=sink_recv.at[source],
            device_id={"ctx": target},
            device_id_type=MESH,
        )

    for target in mates + across:
        share(target, me).start()
    sink_ctx[me] = sink_part[...]
    for target in mates + across:
        share(me, target).wait_recv()
    gathered = sink_ctx[0]
    for source in range(1, n_ctx):
        gathered = gathered + sink_ctx[source]
    for at, ax in enumerate(peers):
        sink_peer[2 * at] = gathered
        swap = pltpu.make_async_remote_copy(
            src_ref=sink_peer.at[2 * at],
            dst_ref=sink_peer.at[2 * at + 1],
            send_sem=peer_send.at[at],
            recv_sem=peer_recv.at[at],
            device_id={ax: 1 - lax.axis_index(ax)},
            device_id_type=MESH,
        )
        swap.start()
        swap.wait()
        gathered = gathered + sink_peer[2 * at + 1]
    gs_ref[...] = gathered

    def finish(h, carry):
        each(h, mates, give, "arrived")

        @pl.when(is_first)
        def _():
            each(h, across, give, "arrived")
            for p in range(parts):
                for home, out in ((key_home, gk_ref), (val_home, gv_ref)):
                    a = home[h, slot * parts + p].astype(jnp.float32)
                    b = home[h, other * parts + p].astype(jnp.float32)
                    out[:, cols(p * hpd + h)] = (a + b).astype(jnp.bfloat16)

        @pl.when(jnp.logical_not(is_first))
        def _():
            for p in range(parts):
                for home, out in ((key_home, gk_ref), (val_home, gv_ref)):
                    out[:, cols(p * hpd + h)] = home[h, slot * parts + p]
        return carry

    lax.fori_loop(0, hpd, finish, 0)

    def drain(h, carry):
        @pl.when(is_first)
        def _():
            each(h, across, fetch, "sent")

        @pl.when(jnp.logical_not(is_first))
        def _():
            each(h, across, give, "sent")
        each(h, mates, fetch, "sent")
        each(h, mates, give, "sent")
        return carry

    lax.fori_loop(0, hpd, drain, 0)
    for target in mates + across:
        share(target, me).wait_send()


def two_block_call(first, parts, hpd, q, g, k, v, chosen, sink):
    unit = k.shape[0]
    block = parts * unit
    n_ctx = 2 * parts
    vmem = pl.BlockSpec(memory_space=pltpu.VMEM)
    smem = pl.BlockSpec(memory_space=pltpu.SMEM)
    slots = pltpu.VMEM((hpd, n_ctx, unit, DH), jnp.bfloat16)
    sums = pltpu.VMEM((2, block, DH), jnp.float32)
    dma = pltpu.SemaphoreType.DMA
    bf16 = jnp.bfloat16
    return pl.pallas_call(
        functools.partial(two_block_kernel, first, parts, hpd, unit),
        out_shape=(
            jax.ShapeDtypeStruct(q.shape, bf16),
            jax.ShapeDtypeStruct(q.shape, bf16),
            jax.ShapeDtypeStruct(k.shape, bf16),
            jax.ShapeDtypeStruct(k.shape, bf16),
            jax.ShapeDtypeStruct((8, DH), jnp.float32),
        ),
        in_specs=[vmem, vmem, vmem, vmem, smem, smem],
        out_specs=(vmem,) * 5,
        scratch_shapes=[
            slots, slots, slots, slots, slots, slots, sums, sums,
            pltpu.VMEM((8, DH), jnp.float32),
            pltpu.VMEM((n_ctx, 8, DH), jnp.float32),
            pltpu.VMEM((4, 8, DH), jnp.float32),
            dma((2, hpd, n_ctx)), dma((2, hpd, n_ctx)),
            dma((2, hpd, n_ctx)), dma((2, hpd, n_ctx)),
            dma((n_ctx,)), dma((n_ctx,)), dma((2,)), dma((2,)),
        ],
        compiler_params=pltpu.CompilerParams(
            collective_id=first, has_side_effects=True, vmem_limit_bytes=40 * 1024 * 1024
        ),
        name=f"two_block_{first}",
    )(q, g, k, v, chosen, sink)


def two_block_body(query, key, value, grad_out, chosen, placed, sink):
    block = query.shape[3]
    unit = key.shape[1]
    parts = block // unit
    hpd = query.shape[4] // DH
    q = query.reshape(block, hpd * DH)
    g = grad_out.reshape(block, hpd * DH)
    k = key.reshape(unit, -1)
    v = value.reshape(unit, -1)
    att, gq, gk, gv, gs = lax.cond(
        placed[0] == 0,
        functools.partial(two_block_call, 0, parts, hpd),
        functools.partial(two_block_call, 1, parts, hpd),
        q, g, k, v, chosen, sink,
    )
    return (
        att.reshape(query.shape),
        gq.reshape(query.shape),
        gk.reshape(key.shape),
        gv.reshape(key.shape),
        gs[0, :HEADS],
    )


def body(query, key, value, grad_out, chosen, placed, sink):
    parts = query.shape[3] // key.shape[1]
    if query.shape[0] == 1 and lax.axis_size("ctx") == 2 * parts:
        return two_block_body(query, key, value, grad_out, chosen, placed, sink)
    return general_body(query, key, value, grad_out, chosen, placed, sink)


def solution(mesh):
    in_specs = (
        P("dp", "ctx", "head", None, None),
        P("dp", "ctx", "head"),
        P("dp", "ctx", "head"),
        P("dp", "ctx", "head", None, None),
        P("dp", None, "head", None),
        P(),
        P("head"),
    )
    out_specs = (
        P("dp", "ctx", "head", None, None),
        P("dp", "ctx", "head", None, None),
        P("dp", "ctx", "head"),
        P("dp", "ctx", "head"),
        P(),
    )
    return jax.shard_map(body, mesh=mesh, in_specs=in_specs, out_specs=out_specs, check_vma=False)
```

```python
import functools
import math

import jax
import jax.numpy as jnp
from jax import lax
from jax.experimental import pallas as pl
from jax.experimental.pallas import tpu as pltpu
from jax.sharding import PartitionSpec as P

HEADS = 32
DH = 128


def inner_rows(left, right):
    return lax.dot_general(
        left, right, (((1,), (1,)), ((), ())), preferred_element_type=jnp.float32
    )


def outer_rows(left, right):
    return lax.dot_general(
        left, right, (((0,), (0,)), ((), ())), preferred_element_type=jnp.float32
    )


def attend_block(query_rows, grad_rows, tiles, usable, sink_logit):
    rows, width = query_rows.shape
    scale = 1.0 / math.sqrt(width)
    keys = tiles[:, :, :width].reshape(-1, width)
    vals = tiles[:, :, width:].reshape(-1, width)
    scores = inner_rows(query_rows, keys) * scale
    cols = tiles.shape[0] * rows
    tile_of = jnp.arange(cols) // rows
    offset = jnp.arange(cols) % rows
    own_ok = offset[None, :] <= jnp.arange(rows)[:, None]
    allowed = jnp.where(tile_of[None, :] == 0, own_ok, usable[tile_of][None, :])
    masked = jnp.where(allowed, scores, -jnp.inf)
    top = jnp.maximum(jnp.max(masked, axis=1), sink_logit)
    expo = jnp.exp(masked - top[:, None])
    sink_part = jnp.exp(sink_logit - top)
    total = sink_part + jnp.sum(expo, axis=1)
    prob = expo / total[:, None]
    weights = prob.astype(jnp.bfloat16)
    attended = jnp.dot(weights, vals, preferred_element_type=jnp.float32).astype(jnp.bfloat16)
    stored = lax.optimization_barrier(attended)
    delta = jnp.sum(grad_rows.astype(jnp.float32) * stored.astype(jnp.float32), axis=1)
    dprob = inner_rows(grad_rows, vals)
    dscore = (prob * (dprob - delta[:, None]) * scale).astype(jnp.bfloat16)
    grad_query = jnp.dot(dscore, keys, preferred_element_type=jnp.float32).astype(jnp.bfloat16)
    grad_keys = outer_rows(dscore, query_rows).astype(jnp.bfloat16)
    grad_vals = outer_rows(weights, grad_rows).astype(jnp.bfloat16)
    tiles_grad = jnp.concatenate([grad_keys, grad_vals], axis=1).reshape(tiles.shape)
    sink_grad = -jnp.sum(sink_part / total * delta)
    return (attended, grad_query, tiles_grad, sink_grad)


def general_body(query, key, value, grad_out, chosen, placed, sink):
    seqs = query.shape[0]
    block = query.shape[3]
    width = DH
    hpd = query.shape[4] // width
    unit = key.shape[1]
    parts_per = block // unit
    n_ctx = lax.axis_size("ctx")
    nblk = n_ctx // parts_per
    place = lax.axis_index("ctx")
    slot = place // parts_per
    position = place % parts_per
    slots = jnp.arange(nblk, dtype=jnp.int32)
    seq_block = jnp.sum(jnp.where(slots == slot, placed, 0))
    slot_of = jnp.sum(jnp.where(placed[None, :] == slots[:, None], slots[None, :], 0), axis=1)
    mine = lax.dynamic_slice_in_dim(chosen, seq_block, 1, 1)[:, 0]
    mine = lax.dynamic_slice_in_dim(mine, position * hpd, hpd, 1)
    usable_pick = mine < seq_block
    mapped = jnp.sum(jnp.where(mine[..., None] == slots, slot_of, 0), axis=-1)
    mapped = jnp.where(usable_pick, mapped, slot)
    lead = jnp.broadcast_to(slot, mine.shape[:2] + (1,))
    picks = jnp.concatenate([lead, mapped], axis=-1)
    kinds = picks.shape[-1]
    usable = jnp.concatenate([jnp.ones(mine.shape[:2] + (1,), bool), usable_pick], axis=-1)
    sink_mine = lax.dynamic_slice_in_dim(sink, position * hpd, hpd)
    paired = jnp.concatenate(
        [
            key.reshape(seqs, unit, parts_per, hpd, width),
            value.reshape(seqs, unit, parts_per, hpd, width),
        ],
        axis=-1,
    )
    paired = jnp.transpose(paired, (2, 0, 3, 1, 4))
    items = seqs * hpd
    frag = unit * 2 * width // n_ctx
    seq_ix = jnp.arange(seqs, dtype=jnp.int32)[None, :, None, None, None]
    head_ix = jnp.arange(hpd, dtype=jnp.int32)[None, None, :, None, None]
    spread = jnp.transpose(paired.reshape(parts_per, seqs, hpd, n_ctx, frag), (3, 0, 1, 2, 4))
    held = lax.all_to_all(spread, "ctx", split_axis=0, concat_axis=0, tiled=True)
    held = jnp.transpose(held, (2, 3, 0, 1, 4)).reshape(seqs, hpd, n_ctx * parts_per, frag)
    match_block = placed[:, None] == slots[None, :]
    chosen_all = jnp.sum(jnp.where(match_block[None, :, :, None, None], chosen[:, None], 0), axis=2)
    before = chosen_all < placed[None, :, None, None]
    mapped_all = jnp.sum(jnp.where(chosen_all[..., None] == slots, slot_of, 0), axis=-1)
    own_slot = slots[None, :, None, None]
    mapped_all = jnp.where(before, mapped_all, own_slot)
    lead_all = jnp.broadcast_to(own_slot, mapped_all.shape[:3] + (1,))
    picks_all = jnp.concatenate([lead_all, mapped_all], axis=-1)
    picks_all = jnp.transpose(
        picks_all.reshape(seqs, nblk, parts_per, hpd, kinds), (1, 2, 0, 3, 4)
    ).reshape(n_ctx, seqs, hpd, kinds)
    dest_group = (jnp.arange(n_ctx, dtype=jnp.int32) % parts_per)[:, None, None, None, None]
    part_ids = jnp.arange(parts_per, dtype=jnp.int32)[None, None, None, None, :]
    route = (picks_all[..., None] * parts_per + part_ids) * parts_per + dest_group
    outgoing = held[seq_ix, head_ix, route]
    fetched = lax.all_to_all(outgoing, "ctx", split_axis=0, concat_axis=0, tiled=True)
    tiles_items = jnp.transpose(fetched, (1, 2, 3, 4, 0, 5)).reshape(
        items, kinds, parts_per * unit, 2 * width
    )
    query_heads = jnp.transpose(query.reshape(seqs, block, hpd, width), (0, 2, 1, 3)).reshape(
        items, block, width
    )
    grad_heads = jnp.transpose(grad_out.reshape(seqs, block, hpd, width), (0, 2, 1, 3)).reshape(
        items, block, width
    )
    sink_items = jnp.tile(sink_mine, seqs)

    def per_head(item):
        q_rows, g_rows, tiles, use_row, sink_logit = item
        return attend_block(q_rows, g_rows, tiles, use_row, sink_logit)

    atts, grads_q, tiles_grad, sink_grads = lax.map(
        per_head, (query_heads, grad_heads, tiles_items, usable.reshape(items, -1), sink_items)
    )
    attended = jnp.transpose(atts.reshape(seqs, hpd, block, width), (0, 2, 1, 3)).reshape(
        seqs, 1, 1, block, hpd * width
    )
    grad_query = jnp.transpose(grads_q.reshape(seqs, hpd, block, width), (0, 2, 1, 3)).reshape(
        seqs, 1, 1, block, hpd * width
    )
    shards = tiles_grad.reshape(seqs, hpd, kinds, parts_per, n_ctx, frag)
    sendback = jnp.transpose(shards, (4, 0, 1, 2, 3, 5))
    landed = lax.all_to_all(sendback, "ctx", split_axis=0, concat_axis=0, tiled=True)
    pooled = (
        jnp.zeros((seqs, hpd, n_ctx * parts_per, frag), jnp.float32)
        .at[seq_ix, head_ix, route]
        .add(landed.astype(jnp.float32))
    )
    pooled = jnp.transpose(pooled.reshape(seqs, hpd, n_ctx, parts_per, frag), (2, 3, 0, 1, 4))
    homed = lax.all_to_all(
        pooled.astype(jnp.bfloat16), "ctx", split_axis=0, concat_axis=0, tiled=True
    ).astype(pooled.dtype)
    totals = jnp.transpose(homed, (1, 2, 3, 0, 4)).reshape(parts_per, seqs, hpd, unit, 2 * width)
    totals = jnp.transpose(totals, (1, 3, 0, 2, 4))
    grad_key = totals[..., :width].reshape(seqs, unit, parts_per * hpd * width).astype(jnp.bfloat16)
    grad_value = (
        totals[..., width:].reshape(seqs, unit, parts_per * hpd * width).astype(jnp.bfloat16)
    )
    sink_local = jnp.sum(sink_grads.reshape(seqs, hpd), axis=0)
    start = lax.axis_index("head") * (parts_per * hpd) + position * hpd
    spread_sink = lax.dynamic_update_slice(jnp.zeros((HEADS,), jnp.float32), sink_local, (start,))
    grad_sink = lax.psum(spread_sink, ("dp", "ctx", "head"))
    return (attended, grad_query, grad_key, grad_value, grad_sink)


MESH = pl.DeviceIdType.MESH
ROWS = 256


def two_block_kernel(
    first, parts, hpd, unit,
    q_ref, g_ref, k_ref, v_ref, chosen_ref, sink_ref,
    att_ref, gq_ref, gk_ref, gv_ref, gs_ref,
    keys, vals, key_part, val_part, key_home, val_home, key_sum, val_sum,
    sink_part, sink_ctx, sink_peer,
    in_send, in_recv, out_send, out_recv, sink_send, sink_recv, peer_send, peer_recv,
):
    width = DH
    block = parts * unit
    scale = 1.0 / math.sqrt(width)
    me = lax.axis_index("ctx")
    slot = me // parts
    pos = me % parts
    other = 1 - slot
    is_first = slot == first
    n_ctx = 2 * parts
    mates = [slot * parts + (pos + d) % parts for d in range(1, parts)]
    across = [other * parts + (pos + d) % parts for d in range(parts)]
    peers = [ax for ax in ("head", "dp") if lax.axis_size(ax) > 1]

    barrier = pltpu.get_barrier_semaphore()
    for target in mates + across:
        pl.semaphore_signal(barrier, inc=1, device_id={"ctx": target}, device_id_type=MESH)
    for ax in peers:
        pl.semaphore_signal(barrier, inc=1, device_id={ax: 1 - lax.axis_index(ax)}, device_id_type=MESH)
    pl.semaphore_wait(barrier, n_ctx - 1 + len(peers))

    def cols(at):
        return pl.ds(pl.multiple_of(at * width, width), width)

    def fetch(h, target, source, which):
        src = (k_ref, v_ref)[which]
        dst = (keys, vals)[which]
        return pltpu.make_async_remote_copy(
            src_ref=src.at[:, cols((target % parts) * hpd + h)],
            dst_ref=dst.at[h, source],
            send_sem=in_send.at[which, h, target],
            recv_sem=in_recv.at[which, h, source],
            device_id={"ctx": target},
            device_id_type=MESH,
        )

    def give(h, target, source, which):
        src = (key_part, val_part)[which]
        dst = (key_home, val_home)[which]
        return pltpu.make_async_remote_copy(
            src_ref=src.at[h, target],
            dst_ref=dst.at[h, source],
            send_sem=out_send.at[which, h, target],
            recv_sem=out_recv.at[which, h, source],
            device_id={"ctx": target},
            device_id_type=MESH,
        )

    def each(h, targets, make, act):
        for target in targets:
            for which in range(2):
                if act == "start":
                    make(h, target, me, which).start()
                elif act == "sent":
                    make(h, target, me, which).wait_send()
                else:
                    make(h, me, target, which).wait_recv()

    @pl.when(is_first)
    def _():
        each(0, across, fetch, "start")

    def send_head(h, carry):
        each(h, mates, fetch, "start")
        keys[h, me] = k_ref[:, cols(pos * hpd + h)]
        vals[h, me] = v_ref[:, cols(pos * hpd + h)]
        return carry

    lax.fori_loop(0, hpd, send_head, 0)

    lane = lax.broadcasted_iota(jnp.int32, (8, width), 1)
    top_row = lax.broadcasted_iota(jnp.int32, (8, width), 0) == 0
    sink_part[...] = jnp.zeros((8, width), jnp.float32)

    def attend(h, with_other):
        local_head = pos * hpd + h
        k_own = keys[h, pl.ds(slot * parts, parts)].reshape(block, width)
        v_own = vals[h, pl.ds(slot * parts, parts)].reshape(block, width)
        sink_logit = sink_ref[local_head]
        segs = [(k_own, v_own, 0)]
        if with_other:
            k_oth = keys[h, pl.ds(other * parts, parts)].reshape(block, width)
            v_oth = vals[h, pl.ds(other * parts, parts)].reshape(block, width)
            segs.append((k_oth, v_oth, 1))
            sees = chosen_ref[0, 1, local_head, 0] < 1
            for entry in range(1, chosen_ref.shape[3]):
                sees = jnp.logical_or(sees, chosen_ref[0, 1, local_head, entry] < 1)
            hide = jnp.where(sees, 0.0, -jnp.inf).astype(jnp.float32)
        sink_total = jnp.zeros((1, 1), jnp.float32)
        for r in range(block // ROWS):
            rows = pl.ds(r * ROWS, ROWS)
            q = q_ref[rows, cols(h)]
            g = g_ref[rows, cols(h)]
            used = []
            top = jnp.full((ROWS, 1), sink_logit, jnp.float32)
            for k_all, v_all, kind in segs:
                n = (r + 1) * ROWS if kind == 0 else block
                k, v = k_all[:n], v_all[:n]
                s = inner_rows(q, k) * scale
                if kind == 0:
                    at_row = lax.broadcasted_iota(jnp.int32, (ROWS, n), 0) + r * ROWS
                    at_col = lax.broadcasted_iota(jnp.int32, (ROWS, n), 1)
                    s = jnp.where(at_col <= at_row, s, -jnp.inf)
                else:
                    s = s + hide
                top = jnp.maximum(top, jnp.max(s, axis=1, keepdims=True))
                used.append((k, v, s, kind, n))
            sink_exp = jnp.exp(sink_logit - top)
            total = sink_exp
            expos = []
            for k, v, s, kind, n in used:
                e = jnp.exp(s - top)
                total = total + jnp.sum(e, axis=1, keepdims=True)
                expos.append(e)
            inv = 1.0 / total
            out = jnp.zeros((ROWS, width), jnp.float32)
            probs, weights = [], []
            for (k, v, s, kind, n), e in zip(used, expos):
                p = e * inv
                w = p.astype(jnp.bfloat16)
                out = out + jnp.dot(w, v, preferred_element_type=jnp.float32)
                probs.append(p)
                weights.append(w)
            out = out.astype(jnp.bfloat16)
            att_ref[rows, cols(h)] = out
            delta = jnp.sum(g.astype(jnp.float32) * out.astype(jnp.float32), axis=1, keepdims=True)
            sink_total = sink_total - jnp.sum(sink_exp * inv * delta, axis=0, keepdims=True)
            gq = jnp.zeros((ROWS, width), jnp.float32)
            for (k, v, s, kind, n), p, w in zip(used, probs, weights):
                dprob = inner_rows(g, v)
                ds = (p * (dprob - delta) * scale).astype(jnp.bfloat16)
                gq = gq + jnp.dot(ds, k, preferred_element_type=jnp.float32)
                dk = outer_rows(ds, q)
                dv = outer_rows(w, g)
                if r == 0:
                    key_sum[kind, :n] = dk
                    val_sum[kind, :n] = dv
                    if n < block:
                        key_sum[kind, n:] = jnp.zeros((block - n, width), jnp.float32)
                        val_sum[kind, n:] = jnp.zeros((block - n, width), jnp.float32)
                else:
                    key_sum[kind, :n] += dk
                    val_sum[kind, :n] += dv
            gq_ref[rows, cols(h)] = gq.astype(jnp.bfloat16)
        mine = jnp.logical_and(lane == lax.axis_index("head") * (parts * hpd) + local_head, top_row)
        sink_part[...] += jnp.where(mine, sink_total, 0.0)
        for kind, place in ((0, slot), (1, other))[: 2 if with_other else 1]:
            at = pl.ds(place * parts, parts)
            key_part[h, at] = key_sum[kind].astype(jnp.bfloat16).reshape(parts, unit, width)
            val_part[h, at] = val_sum[kind].astype(jnp.bfloat16).reshape(parts, unit, width)

    def head_step(h, carry):
        @pl.when(jnp.logical_and(is_first, h < hpd - 1))
        def _():
            for target in across:
                for which in range(2):
                    fetch(h, target, me, which).wait_send()
                    fetch(h + 1, target, me, which).start()

        each(h, mates, fetch, "arrived")

        @pl.when(is_first)
        def _():
            attend(h, False)

        @pl.when(jnp.logical_not(is_first))
        def _():
            each(h, across, fetch, "arrived")
            attend(h, True)
            each(h, across, give, "start")

        each(h, mates, give, "start")
        key_home[h, me] = key_part[h, me]
        val_home[h, me] = val_part[h, me]
        return carry

    lax.fori_loop(0, hpd, head_step, 0)

    def share(target, source):
        return pltpu.make_async_remote_copy(
            src_ref=sink_part,
            dst_ref=sink_ctx.at[source],
            send_sem=sink_send.at[target],
            recv_sem=sink_recv.at[source],
            device_id={"ctx": target},
            device_id_type=MESH,
        )

    for target in mates + across:
        share(target, me).start()
    sink_ctx[me] = sink_part[...]
    for target in mates + across:
        share(me, target).wait_recv()
    gathered = sink_ctx[0]
    for source in range(1, n_ctx):
        gathered = gathered + sink_ctx[source]
    for at, ax in enumerate(peers):
        sink_peer[2 * at] = gathered
        swap = pltpu.make_async_remote_copy(
            src_ref=sink_peer.at[2 * at],
            dst_ref=sink_peer.at[2 * at + 1],
            send_sem=peer_send.at[at],
            recv_sem=peer_recv.at[at],
            device_id={ax: 1 - lax.axis_index(ax)},
            device_id_type=MESH,
        )
        swap.start()
        swap.wait()
        gathered = gathered + sink_peer[2 * at + 1]
    gs_ref[...] = gathered

    def finish(h, carry):
        each(h, mates, give, "arrived")

        @pl.when(is_first)
        def _():
            each(h, across, give, "arrived")
            for p in range(parts):
                for home, out in ((key_home, gk_ref), (val_home, gv_ref)):
                    a = home[h, slot * parts + p].astype(jnp.float32)
                    b = home[h, other * parts + p].astype(jnp.float32)
                    out[:, cols(p * hpd + h)] = (a + b).astype(jnp.bfloat16)

        @pl.when(jnp.logical_not(is_first))
        def _():
            for p in range(parts):
                for home, out in ((key_home, gk_ref), (val_home, gv_ref)):
                    out[:, cols(p * hpd + h)] = home[h, slot * parts + p]
        return carry

    lax.fori_loop(0, hpd, finish, 0)

    def drain(h, carry):
        @pl.when(jnp.logical_and(is_first, h == hpd - 1))
        def _():
            each(h, across, fetch, "sent")

        @pl.when(jnp.logical_not(is_first))
        def _():
            each(h, across, give, "sent")
        each(h, mates, fetch, "sent")
        each(h, mates, give, "sent")
        return carry

    lax.fori_loop(0, hpd, drain, 0)
    for target in mates + across:
        share(target, me).wait_send()


def two_block_call(first, parts, hpd, q, g, k, v, chosen, sink):
    unit = k.shape[0]
    block = parts * unit
    n_ctx = 2 * parts
    vmem = pl.BlockSpec(memory_space=pltpu.VMEM)
    smem = pl.BlockSpec(memory_space=pltpu.SMEM)
    slots = pltpu.VMEM((hpd, n_ctx, unit, DH), jnp.bfloat16)
    sums = pltpu.VMEM((2, block, DH), jnp.float32)
    dma = pltpu.SemaphoreType.DMA
    bf16 = jnp.bfloat16
    return pl.pallas_call(
        functools.partial(two_block_kernel, first, parts, hpd, unit),
        out_shape=(
            jax.ShapeDtypeStruct(q.shape, bf16),
            jax.ShapeDtypeStruct(q.shape, bf16),
            jax.ShapeDtypeStruct(k.shape, bf16),
            jax.ShapeDtypeStruct(k.shape, bf16),
            jax.ShapeDtypeStruct((8, DH), jnp.float32),
        ),
        in_specs=[vmem, vmem, vmem, vmem, smem, smem],
        out_specs=(vmem,) * 5,
        scratch_shapes=[
            slots, slots, slots, slots, slots, slots, sums, sums,
            pltpu.VMEM((8, DH), jnp.float32),
            pltpu.VMEM((n_ctx, 8, DH), jnp.float32),
            pltpu.VMEM((4, 8, DH), jnp.float32),
            dma((2, hpd, n_ctx)), dma((2, hpd, n_ctx)),
            dma((2, hpd, n_ctx)), dma((2, hpd, n_ctx)),
            dma((n_ctx,)), dma((n_ctx,)), dma((2,)), dma((2,)),
        ],
        compiler_params=pltpu.CompilerParams(
            collective_id=first, has_side_effects=True, vmem_limit_bytes=40 * 1024 * 1024
        ),
        name=f"two_block_{first}",
    )(q, g, k, v, chosen, sink)


def put_kernel(n, *refs):
    sems = refs[-1]
    copies = [pltpu.make_async_copy(refs[i], refs[n + i], sems.at[i]) for i in range(n)]
    for copy in copies:
        copy.start()
    for copy in copies:
        copy.wait()


def put_results(*arrays):
    n = len(arrays)
    anywhere = pl.BlockSpec(memory_space=pl.ANY)
    return pl.pallas_call(
        functools.partial(put_kernel, n),
        out_shape=tuple(jax.ShapeDtypeStruct(a.shape, a.dtype) for a in arrays),
        in_specs=[anywhere] * n,
        out_specs=(anywhere,) * n,
        scratch_shapes=[pltpu.SemaphoreType.DMA((n,))],
        name="put_results",
    )(*arrays)


def two_block_body(query, key, value, grad_out, chosen, placed, sink):
    block = query.shape[3]
    unit = key.shape[1]
    parts = block // unit
    hpd = query.shape[4] // DH
    q = query.reshape(block, hpd * DH)
    g = grad_out.reshape(block, hpd * DH)
    k = key.reshape(unit, -1)
    v = value.reshape(unit, -1)
    att, gq, gk, gv, gs = lax.cond(
        placed[0] == 0,
        functools.partial(two_block_call, 0, parts, hpd),
        functools.partial(two_block_call, 1, parts, hpd),
        q, g, k, v, chosen, sink,
    )
    att, gq, gk, gv = put_results(att, gq, gk, gv)
    return (
        att.reshape(query.shape),
        gq.reshape(query.shape),
        gk.reshape(key.shape),
        gv.reshape(key.shape),
        gs[0, :HEADS],
    )


def body(query, key, value, grad_out, chosen, placed, sink):
    parts = query.shape[3] // key.shape[1]
    if query.shape[0] == 1 and lax.axis_size("ctx") == 2 * parts:
        return two_block_body(query, key, value, grad_out, chosen, placed, sink)
    return general_body(query, key, value, grad_out, chosen, placed, sink)


def solution(mesh):
    in_specs = (
        P("dp", "ctx", "head", None, None),
        P("dp", "ctx", "head"),
        P("dp", "ctx", "head"),
        P("dp", "ctx", "head", None, None),
        P("dp", None, "head", None),
        P(),
        P("head"),
    )
    out_specs = (
        P("dp", "ctx", "head", None, None),
        P("dp", "ctx", "head", None, None),
        P("dp", "ctx", "head"),
        P("dp", "ctx", "head"),
        P(),
    )
    return jax.shard_map(body, mesh=mesh, in_specs=in_specs, out_specs=out_specs, check_vma=False)
```

```python
import functools
import math

import jax
import jax.numpy as jnp
from jax import lax
from jax.experimental import pallas as pl
from jax.experimental.pallas import tpu as pltpu
from jax.sharding import PartitionSpec as P

HEADS = 32
DH = 128


def inner_rows(left, right):
    return lax.dot_general(
        left, right, (((1,), (1,)), ((), ())), preferred_element_type=jnp.float32
    )


def outer_rows(left, right):
    return lax.dot_general(
        left, right, (((0,), (0,)), ((), ())), preferred_element_type=jnp.float32
    )


def attend_block(query_rows, grad_rows, tiles, usable, sink_logit):
    rows, width = query_rows.shape
    scale = 1.0 / math.sqrt(width)
    keys = tiles[:, :, :width].reshape(-1, width)
    vals = tiles[:, :, width:].reshape(-1, width)
    scores = inner_rows(query_rows, keys) * scale
    cols = tiles.shape[0] * rows
    tile_of = jnp.arange(cols) // rows
    offset = jnp.arange(cols) % rows
    own_ok = offset[None, :] <= jnp.arange(rows)[:, None]
    allowed = jnp.where(tile_of[None, :] == 0, own_ok, usable[tile_of][None, :])
    masked = jnp.where(allowed, scores, -jnp.inf)
    top = jnp.maximum(jnp.max(masked, axis=1), sink_logit)
    expo = jnp.exp(masked - top[:, None])
    sink_part = jnp.exp(sink_logit - top)
    total = sink_part + jnp.sum(expo, axis=1)
    prob = expo / total[:, None]
    weights = prob.astype(jnp.bfloat16)
    attended = jnp.dot(weights, vals, preferred_element_type=jnp.float32).astype(jnp.bfloat16)
    stored = lax.optimization_barrier(attended)
    delta = jnp.sum(grad_rows.astype(jnp.float32) * stored.astype(jnp.float32), axis=1)
    dprob = inner_rows(grad_rows, vals)
    dscore = (prob * (dprob - delta[:, None]) * scale).astype(jnp.bfloat16)
    grad_query = jnp.dot(dscore, keys, preferred_element_type=jnp.float32).astype(jnp.bfloat16)
    grad_keys = outer_rows(dscore, query_rows).astype(jnp.bfloat16)
    grad_vals = outer_rows(weights, grad_rows).astype(jnp.bfloat16)
    tiles_grad = jnp.concatenate([grad_keys, grad_vals], axis=1).reshape(tiles.shape)
    sink_grad = -jnp.sum(sink_part / total * delta)
    return (attended, grad_query, tiles_grad, sink_grad)


def general_body(query, key, value, grad_out, chosen, placed, sink):
    seqs = query.shape[0]
    block = query.shape[3]
    width = DH
    hpd = query.shape[4] // width
    unit = key.shape[1]
    parts_per = block // unit
    n_ctx = lax.axis_size("ctx")
    nblk = n_ctx // parts_per
    place = lax.axis_index("ctx")
    slot = place // parts_per
    position = place % parts_per
    slots = jnp.arange(nblk, dtype=jnp.int32)
    seq_block = jnp.sum(jnp.where(slots == slot, placed, 0))
    slot_of = jnp.sum(jnp.where(placed[None, :] == slots[:, None], slots[None, :], 0), axis=1)
    mine = lax.dynamic_slice_in_dim(chosen, seq_block, 1, 1)[:, 0]
    mine = lax.dynamic_slice_in_dim(mine, position * hpd, hpd, 1)
    usable_pick = mine < seq_block
    mapped = jnp.sum(jnp.where(mine[..., None] == slots, slot_of, 0), axis=-1)
    mapped = jnp.where(usable_pick, mapped, slot)
    lead = jnp.broadcast_to(slot, mine.shape[:2] + (1,))
    picks = jnp.concatenate([lead, mapped], axis=-1)
    kinds = picks.shape[-1]
    usable = jnp.concatenate([jnp.ones(mine.shape[:2] + (1,), bool), usable_pick], axis=-1)
    sink_mine = lax.dynamic_slice_in_dim(sink, position * hpd, hpd)
    paired = jnp.concatenate(
        [
            key.reshape(seqs, unit, parts_per, hpd, width),
            value.reshape(seqs, unit, parts_per, hpd, width),
        ],
        axis=-1,
    )
    paired = jnp.transpose(paired, (2, 0, 3, 1, 4))
    items = seqs * hpd
    frag = unit * 2 * width // n_ctx
    seq_ix = jnp.arange(seqs, dtype=jnp.int32)[None, :, None, None, None]
    head_ix = jnp.arange(hpd, dtype=jnp.int32)[None, None, :, None, None]
    spread = jnp.transpose(paired.reshape(parts_per, seqs, hpd, n_ctx, frag), (3, 0, 1, 2, 4))
    held = lax.all_to_all(spread, "ctx", split_axis=0, concat_axis=0, tiled=True)
    held = jnp.transpose(held, (2, 3, 0, 1, 4)).reshape(seqs, hpd, n_ctx * parts_per, frag)
    match_block = placed[:, None] == slots[None, :]
    chosen_all = jnp.sum(jnp.where(match_block[None, :, :, None, None], chosen[:, None], 0), axis=2)
    before = chosen_all < placed[None, :, None, None]
    mapped_all = jnp.sum(jnp.where(chosen_all[..., None] == slots, slot_of, 0), axis=-1)
    own_slot = slots[None, :, None, None]
    mapped_all = jnp.where(before, mapped_all, own_slot)
    lead_all = jnp.broadcast_to(own_slot, mapped_all.shape[:3] + (1,))
    picks_all = jnp.concatenate([lead_all, mapped_all], axis=-1)
    picks_all = jnp.transpose(
        picks_all.reshape(seqs, nblk, parts_per, hpd, kinds), (1, 2, 0, 3, 4)
    ).reshape(n_ctx, seqs, hpd, kinds)
    dest_group = (jnp.arange(n_ctx, dtype=jnp.int32) % parts_per)[:, None, None, None, None]
    part_ids = jnp.arange(parts_per, dtype=jnp.int32)[None, None, None, None, :]
    route = (picks_all[..., None] * parts_per + part_ids) * parts_per + dest_group
    outgoing = held[seq_ix, head_ix, route]
    fetched = lax.all_to_all(outgoing, "ctx", split_axis=0, concat_axis=0, tiled=True)
    tiles_items = jnp.transpose(fetched, (1, 2, 3, 4, 0, 5)).reshape(
        items, kinds, parts_per * unit, 2 * width
    )
    query_heads = jnp.transpose(query.reshape(seqs, block, hpd, width), (0, 2, 1, 3)).reshape(
        items, block, width
    )
    grad_heads = jnp.transpose(grad_out.reshape(seqs, block, hpd, width), (0, 2, 1, 3)).reshape(
        items, block, width
    )
    sink_items = jnp.tile(sink_mine, seqs)

    def per_head(item):
        q_rows, g_rows, tiles, use_row, sink_logit = item
        return attend_block(q_rows, g_rows, tiles, use_row, sink_logit)

    atts, grads_q, tiles_grad, sink_grads = lax.map(
        per_head, (query_heads, grad_heads, tiles_items, usable.reshape(items, -1), sink_items)
    )
    attended = jnp.transpose(atts.reshape(seqs, hpd, block, width), (0, 2, 1, 3)).reshape(
        seqs, 1, 1, block, hpd * width
    )
    grad_query = jnp.transpose(grads_q.reshape(seqs, hpd, block, width), (0, 2, 1, 3)).reshape(
        seqs, 1, 1, block, hpd * width
    )
    shards = tiles_grad.reshape(seqs, hpd, kinds, parts_per, n_ctx, frag)
    sendback = jnp.transpose(shards, (4, 0, 1, 2, 3, 5))
    landed = lax.all_to_all(sendback, "ctx", split_axis=0, concat_axis=0, tiled=True)
    pooled = (
        jnp.zeros((seqs, hpd, n_ctx * parts_per, frag), jnp.float32)
        .at[seq_ix, head_ix, route]
        .add(landed.astype(jnp.float32))
    )
    pooled = jnp.transpose(pooled.reshape(seqs, hpd, n_ctx, parts_per, frag), (2, 3, 0, 1, 4))
    homed = lax.all_to_all(
        pooled.astype(jnp.bfloat16), "ctx", split_axis=0, concat_axis=0, tiled=True
    ).astype(pooled.dtype)
    totals = jnp.transpose(homed, (1, 2, 3, 0, 4)).reshape(parts_per, seqs, hpd, unit, 2 * width)
    totals = jnp.transpose(totals, (1, 3, 0, 2, 4))
    grad_key = totals[..., :width].reshape(seqs, unit, parts_per * hpd * width).astype(jnp.bfloat16)
    grad_value = (
        totals[..., width:].reshape(seqs, unit, parts_per * hpd * width).astype(jnp.bfloat16)
    )
    sink_local = jnp.sum(sink_grads.reshape(seqs, hpd), axis=0)
    start = lax.axis_index("head") * (parts_per * hpd) + position * hpd
    spread_sink = lax.dynamic_update_slice(jnp.zeros((HEADS,), jnp.float32), sink_local, (start,))
    grad_sink = lax.psum(spread_sink, ("dp", "ctx", "head"))
    return (attended, grad_query, grad_key, grad_value, grad_sink)


MESH = pl.DeviceIdType.MESH
ROWS = 256


def two_block_kernel(
    first, parts, hpd, unit,
    q_ref, g_ref, k_ref, v_ref, chosen_ref, sink_ref,
    att_ref, gq_ref, gk_ref, gv_ref, gs_ref,
    keys, vals, key_part, val_part, key_home, val_home, key_sum, val_sum,
    sink_part, sink_ctx, sink_peer,
    in_send, in_recv, out_send, out_recv, sink_send, sink_recv, peer_send, peer_recv,
):
    width = DH
    block = parts * unit
    scale = 1.0 / math.sqrt(width)
    me = lax.axis_index("ctx")
    slot = me // parts
    pos = me % parts
    other = 1 - slot
    is_first = slot == first
    n_ctx = 2 * parts
    mates = [slot * parts + (pos + d) % parts for d in range(1, parts)]
    across = [other * parts + (pos + d) % parts for d in range(parts)]
    peers = [ax for ax in ("head", "dp") if lax.axis_size(ax) > 1]

    barrier = pltpu.get_barrier_semaphore()
    for target in mates + across:
        pl.semaphore_signal(barrier, inc=1, device_id={"ctx": target}, device_id_type=MESH)
    for ax in peers:
        pl.semaphore_signal(barrier, inc=1, device_id={ax: 1 - lax.axis_index(ax)}, device_id_type=MESH)
    pl.semaphore_wait(barrier, n_ctx - 1 + len(peers))

    def cols(at):
        return pl.ds(pl.multiple_of(at * width, width), width)

    def fetch(h, target, source, which):
        src = (k_ref, v_ref)[which]
        dst = (keys, vals)[which]
        return pltpu.make_async_remote_copy(
            src_ref=src.at[:, cols((target % parts) * hpd + h)],
            dst_ref=dst.at[h, source],
            send_sem=in_send.at[which, h, target],
            recv_sem=in_recv.at[which, h, source],
            device_id={"ctx": target},
            device_id_type=MESH,
        )

    def give(h, target, source, which):
        src = (key_part, val_part)[which]
        dst = (key_home, val_home)[which]
        return pltpu.make_async_remote_copy(
            src_ref=src.at[h, target],
            dst_ref=dst.at[h, source],
            send_sem=out_send.at[which, h, target],
            recv_sem=out_recv.at[which, h, source],
            device_id={"ctx": target},
            device_id_type=MESH,
        )

    def each(h, targets, make, act):
        for target in targets:
            for which in range(2):
                if act == "start":
                    make(h, target, me, which).start()
                elif act == "sent":
                    make(h, target, me, which).wait_send()
                else:
                    make(h, me, target, which).wait_recv()

    half = parts // 2
    pieces = 2 * half
    ahead = pieces - 1

    def piece(h, s):
        visit, which = half - 1 - s // 2, s % 2
        targets = [other * parts + visit * 2 + t for t in range(2)]
        return [fetch(h, target, me, which) for target in targets]

    @pl.when(is_first)
    def _():
        for s in range(ahead):
            for copy in piece(0, s):
                copy.start()

    def send_head(h, carry):
        each(h, mates, fetch, "start")
        keys[h, me] = k_ref[:, cols(pos * hpd + h)]
        vals[h, me] = v_ref[:, cols(pos * hpd + h)]
        return carry

    lax.fori_loop(0, hpd, send_head, 0)

    lane = lax.broadcasted_iota(jnp.int32, (8, width), 1)
    top_row = lax.broadcasted_iota(jnp.int32, (8, width), 0) == 0
    sink_part[...] = jnp.zeros((8, width), jnp.float32)

    def attend(h, with_other):
        local_head = pos * hpd + h
        k_own = keys[h, pl.ds(slot * parts, parts)].reshape(block, width)
        v_own = vals[h, pl.ds(slot * parts, parts)].reshape(block, width)
        sink_logit = sink_ref[local_head]
        segs = [(k_own, v_own, 0)]
        if with_other:
            k_oth = keys[h, pl.ds(other * parts, parts)].reshape(block, width)
            v_oth = vals[h, pl.ds(other * parts, parts)].reshape(block, width)
            segs.append((k_oth, v_oth, 1))
            sees = chosen_ref[0, 1, local_head, 0] < 1
            for entry in range(1, chosen_ref.shape[3]):
                sees = jnp.logical_or(sees, chosen_ref[0, 1, local_head, entry] < 1)
            hide = jnp.where(sees, 0.0, -jnp.inf).astype(jnp.float32)
        sink_total = jnp.zeros((1, 1), jnp.float32)
        for r in range(block // ROWS):
            rows = pl.ds(r * ROWS, ROWS)
            q = q_ref[rows, cols(h)]
            g = g_ref[rows, cols(h)]
            used = []
            top = jnp.full((ROWS, 1), sink_logit, jnp.float32)
            for k_all, v_all, kind in segs:
                n = (r + 1) * ROWS if kind == 0 else block
                k, v = k_all[:n], v_all[:n]
                s = inner_rows(q, k) * scale
                if kind == 0:
                    at_row = lax.broadcasted_iota(jnp.int32, (ROWS, n), 0) + r * ROWS
                    at_col = lax.broadcasted_iota(jnp.int32, (ROWS, n), 1)
                    s = jnp.where(at_col <= at_row, s, -jnp.inf)
                else:
                    s = s + hide
                top = jnp.maximum(top, jnp.max(s, axis=1, keepdims=True))
                used.append((k, v, s, kind, n))
            sink_exp = jnp.exp(sink_logit - top)
            total = sink_exp
            expos = []
            for k, v, s, kind, n in used:
                e = jnp.exp(s - top)
                total = total + jnp.sum(e, axis=1, keepdims=True)
                expos.append(e)
            inv = 1.0 / total
            out = jnp.zeros((ROWS, width), jnp.float32)
            probs, weights = [], []
            for (k, v, s, kind, n), e in zip(used, expos):
                p = e * inv
                w = p.astype(jnp.bfloat16)
                out = out + jnp.dot(w, v, preferred_element_type=jnp.float32)
                probs.append(p)
                weights.append(w)
            out = out.astype(jnp.bfloat16)
            att_ref[rows, cols(h)] = out
            delta = jnp.sum(g.astype(jnp.float32) * out.astype(jnp.float32), axis=1, keepdims=True)
            sink_total = sink_total - jnp.sum(sink_exp * inv * delta, axis=0, keepdims=True)
            gq = jnp.zeros((ROWS, width), jnp.float32)
            for (k, v, s, kind, n), p, w in zip(used, probs, weights):
                dprob = inner_rows(g, v)
                ds = (p * (dprob - delta) * scale).astype(jnp.bfloat16)
                gq = gq + jnp.dot(ds, k, preferred_element_type=jnp.float32)
                dk = outer_rows(ds, q)
                dv = outer_rows(w, g)
                if r == 0:
                    key_sum[kind, :n] = dk
                    val_sum[kind, :n] = dv
                    if n < block:
                        key_sum[kind, n:] = jnp.zeros((block - n, width), jnp.float32)
                        val_sum[kind, n:] = jnp.zeros((block - n, width), jnp.float32)
                else:
                    key_sum[kind, :n] += dk
                    val_sum[kind, :n] += dv
            gq_ref[rows, cols(h)] = gq.astype(jnp.bfloat16)
        mine = jnp.logical_and(lane == lax.axis_index("head") * (parts * hpd) + local_head, top_row)
        sink_part[...] += jnp.where(mine, sink_total, 0.0)
        for kind, place in ((0, slot), (1, other))[: 2 if with_other else 1]:
            at = pl.ds(place * parts, parts)
            key_part[h, at] = key_sum[kind].astype(jnp.bfloat16).reshape(parts, unit, width)
            val_part[h, at] = val_sum[kind].astype(jnp.bfloat16).reshape(parts, unit, width)

    def share(target, source):
        return pltpu.make_async_remote_copy(
            src_ref=sink_part,
            dst_ref=sink_ctx.at[source],
            send_sem=sink_send.at[target],
            recv_sem=sink_recv.at[source],
            device_id={"ctx": target},
            device_id_type=MESH,
        )

    def head_step(h, carry):
        @pl.when(is_first)
        def _():
            for gone, late in zip(piece(h, 0), piece(h, ahead)):
                gone.wait_send()
                late.start()

        @pl.when(jnp.logical_and(is_first, h < hpd - 1))
        def _():
            for s in range(1, pieces):
                for gone, late in zip(piece(h, s), piece(h + 1, s - 1)):
                    gone.wait_send()
                    late.start()

        each(h, mates, fetch, "arrived")

        @pl.when(is_first)
        def _():
            attend(h, False)

        @pl.when(jnp.logical_not(is_first))
        def _():
            each(h, across, fetch, "arrived")
            attend(h, True)

        @pl.when(h == hpd - 1)
        def _():
            for target in mates + across:
                share(target, me).start()

        @pl.when(jnp.logical_not(is_first))
        def _():
            each(h, across, give, "start")

        each(h, mates, give, "start")
        key_home[h, me] = key_part[h, me]
        val_home[h, me] = val_part[h, me]
        return carry

    lax.fori_loop(0, hpd, head_step, 0)

    sink_ctx[me] = sink_part[...]
    for target in mates + across:
        share(me, target).wait_recv()
    gathered = sink_ctx[0]
    for source in range(1, n_ctx):
        gathered = gathered + sink_ctx[source]
    for at, ax in enumerate(peers):
        sink_peer[2 * at] = gathered
        swap = pltpu.make_async_remote_copy(
            src_ref=sink_peer.at[2 * at],
            dst_ref=sink_peer.at[2 * at + 1],
            send_sem=peer_send.at[at],
            recv_sem=peer_recv.at[at],
            device_id={ax: 1 - lax.axis_index(ax)},
            device_id_type=MESH,
        )
        swap.start()
        swap.wait()
        gathered = gathered + sink_peer[2 * at + 1]
    gs_ref[...] = gathered

    def finish(h, carry):
        each(h, mates, give, "arrived")

        @pl.when(is_first)
        def _():
            each(h, across, give, "arrived")
            for p in range(parts):
                for home, out in ((key_home, gk_ref), (val_home, gv_ref)):
                    a = home[h, slot * parts + p].astype(jnp.float32)
                    b = home[h, other * parts + p].astype(jnp.float32)
                    out[:, cols(p * hpd + h)] = (a + b).astype(jnp.bfloat16)

        @pl.when(jnp.logical_not(is_first))
        def _():
            for p in range(parts):
                for home, out in ((key_home, gk_ref), (val_home, gv_ref)):
                    out[:, cols(p * hpd + h)] = home[h, slot * parts + p]
        return carry

    lax.fori_loop(0, hpd, finish, 0)

    def drain(h, carry):
        @pl.when(jnp.logical_and(is_first, h == hpd - 1))
        def _():
            for s in range(1, pieces):
                for copy in piece(h, s):
                    copy.wait_send()

        @pl.when(jnp.logical_not(is_first))
        def _():
            each(h, across, give, "sent")
        each(h, mates, fetch, "sent")
        each(h, mates, give, "sent")
        return carry

    lax.fori_loop(0, hpd, drain, 0)
    for target in mates + across:
        share(target, me).wait_send()


def two_block_call(first, parts, hpd, q, g, k, v, chosen, sink):
    unit = k.shape[0]
    block = parts * unit
    n_ctx = 2 * parts
    vmem = pl.BlockSpec(memory_space=pltpu.VMEM)
    smem = pl.BlockSpec(memory_space=pltpu.SMEM)
    slots = pltpu.VMEM((hpd, n_ctx, unit, DH), jnp.bfloat16)
    sums = pltpu.VMEM((2, block, DH), jnp.float32)
    dma = pltpu.SemaphoreType.DMA
    bf16 = jnp.bfloat16
    return pl.pallas_call(
        functools.partial(two_block_kernel, first, parts, hpd, unit),
        out_shape=(
            jax.ShapeDtypeStruct(q.shape, bf16),
            jax.ShapeDtypeStruct(q.shape, bf16),
            jax.ShapeDtypeStruct(k.shape, bf16),
            jax.ShapeDtypeStruct(k.shape, bf16),
            jax.ShapeDtypeStruct((8, DH), jnp.float32),
        ),
        in_specs=[vmem, vmem, vmem, vmem, smem, smem],
        out_specs=(vmem,) * 5,
        scratch_shapes=[
            slots, slots, slots, slots, slots, slots, sums, sums,
            pltpu.VMEM((8, DH), jnp.float32),
            pltpu.VMEM((n_ctx, 8, DH), jnp.float32),
            pltpu.VMEM((4, 8, DH), jnp.float32),
            dma((2, hpd, n_ctx)), dma((2, hpd, n_ctx)),
            dma((2, hpd, n_ctx)), dma((2, hpd, n_ctx)),
            dma((n_ctx,)), dma((n_ctx,)), dma((2,)), dma((2,)),
        ],
        compiler_params=pltpu.CompilerParams(
            collective_id=first, has_side_effects=True, vmem_limit_bytes=40 * 1024 * 1024
        ),
        name=f"two_block_{first}",
    )(q, g, k, v, chosen, sink)


def put_kernel(n, *refs):
    sems = refs[-1]
    copies = [pltpu.make_async_copy(refs[i], refs[n + i], sems.at[i]) for i in range(n)]
    for copy in copies:
        copy.start()
    for copy in copies:
        copy.wait()


def put_results(*arrays):
    n = len(arrays)
    anywhere = pl.BlockSpec(memory_space=pl.ANY)
    return pl.pallas_call(
        functools.partial(put_kernel, n),
        out_shape=tuple(jax.ShapeDtypeStruct(a.shape, a.dtype) for a in arrays),
        in_specs=[anywhere] * n,
        out_specs=(anywhere,) * n,
        scratch_shapes=[pltpu.SemaphoreType.DMA((n,))],
        name="put_results",
    )(*arrays)


def two_block_body(query, key, value, grad_out, chosen, placed, sink):
    block = query.shape[3]
    unit = key.shape[1]
    parts = block // unit
    hpd = query.shape[4] // DH
    q = query.reshape(block, hpd * DH)
    g = grad_out.reshape(block, hpd * DH)
    k = key.reshape(unit, -1)
    v = value.reshape(unit, -1)
    att, gq, gk, gv, gs = lax.cond(
        placed[0] == 0,
        functools.partial(two_block_call, 0, parts, hpd),
        functools.partial(two_block_call, 1, parts, hpd),
        q, g, k, v, chosen, sink,
    )
    att, gq, gk, gv = put_results(att, gq, gk, gv)
    return (
        att.reshape(query.shape),
        gq.reshape(query.shape),
        gk.reshape(key.shape),
        gv.reshape(key.shape),
        gs[0, :HEADS],
    )


def body(query, key, value, grad_out, chosen, placed, sink):
    parts = query.shape[3] // key.shape[1]
    if query.shape[0] == 1 and lax.axis_size("ctx") == 2 * parts:
        return two_block_body(query, key, value, grad_out, chosen, placed, sink)
    return general_body(query, key, value, grad_out, chosen, placed, sink)


def solution(mesh):
    in_specs = (
        P("dp", "ctx", "head", None, None),
        P("dp", "ctx", "head"),
        P("dp", "ctx", "head"),
        P("dp", "ctx", "head", None, None),
        P("dp", None, "head", None),
        P(),
        P("head"),
    )
    out_specs = (
        P("dp", "ctx", "head", None, None),
        P("dp", "ctx", "head", None, None),
        P("dp", "ctx", "head"),
        P("dp", "ctx", "head"),
        P(),
    )
    return jax.shard_map(body, mesh=mesh, in_specs=in_specs, out_specs=out_specs, check_vma=False)
```

```python
import functools
import math

import jax
import jax.numpy as jnp
from jax import lax
from jax.experimental import pallas as pl
from jax.experimental.pallas import tpu as pltpu
from jax.sharding import PartitionSpec as P

HEADS = 32
DH = 128


def inner_rows(left, right):
    return lax.dot_general(
        left, right, (((1,), (1,)), ((), ())), preferred_element_type=jnp.float32
    )


def outer_rows(left, right):
    return lax.dot_general(
        left, right, (((0,), (0,)), ((), ())), preferred_element_type=jnp.float32
    )


def attend_block(query_rows, grad_rows, tiles, usable, sink_logit):
    rows, width = query_rows.shape
    scale = 1.0 / math.sqrt(width)
    keys = tiles[:, :, :width].reshape(-1, width)
    vals = tiles[:, :, width:].reshape(-1, width)
    scores = inner_rows(query_rows, keys) * scale
    cols = tiles.shape[0] * rows
    tile_of = jnp.arange(cols) // rows
    offset = jnp.arange(cols) % rows
    own_ok = offset[None, :] <= jnp.arange(rows)[:, None]
    allowed = jnp.where(tile_of[None, :] == 0, own_ok, usable[tile_of][None, :])
    masked = jnp.where(allowed, scores, -jnp.inf)
    top = jnp.maximum(jnp.max(masked, axis=1), sink_logit)
    expo = jnp.exp(masked - top[:, None])
    sink_part = jnp.exp(sink_logit - top)
    total = sink_part + jnp.sum(expo, axis=1)
    prob = expo / total[:, None]
    weights = prob.astype(jnp.bfloat16)
    attended = jnp.dot(weights, vals, preferred_element_type=jnp.float32).astype(jnp.bfloat16)
    stored = lax.optimization_barrier(attended)
    delta = jnp.sum(grad_rows.astype(jnp.float32) * stored.astype(jnp.float32), axis=1)
    dprob = inner_rows(grad_rows, vals)
    dscore = (prob * (dprob - delta[:, None]) * scale).astype(jnp.bfloat16)
    grad_query = jnp.dot(dscore, keys, preferred_element_type=jnp.float32).astype(jnp.bfloat16)
    grad_keys = outer_rows(dscore, query_rows).astype(jnp.bfloat16)
    grad_vals = outer_rows(weights, grad_rows).astype(jnp.bfloat16)
    tiles_grad = jnp.concatenate([grad_keys, grad_vals], axis=1).reshape(tiles.shape)
    sink_grad = -jnp.sum(sink_part / total * delta)
    return (attended, grad_query, tiles_grad, sink_grad)


def general_body(query, key, value, grad_out, chosen, placed, sink):
    seqs = query.shape[0]
    block = query.shape[3]
    width = DH
    hpd = query.shape[4] // width
    unit = key.shape[1]
    parts_per = block // unit
    n_ctx = lax.axis_size("ctx")
    nblk = n_ctx // parts_per
    place = lax.axis_index("ctx")
    slot = place // parts_per
    position = place % parts_per
    slots = jnp.arange(nblk, dtype=jnp.int32)
    seq_block = jnp.sum(jnp.where(slots == slot, placed, 0))
    slot_of = jnp.sum(jnp.where(placed[None, :] == slots[:, None], slots[None, :], 0), axis=1)
    mine = lax.dynamic_slice_in_dim(chosen, seq_block, 1, 1)[:, 0]
    mine = lax.dynamic_slice_in_dim(mine, position * hpd, hpd, 1)
    usable_pick = mine < seq_block
    mapped = jnp.sum(jnp.where(mine[..., None] == slots, slot_of, 0), axis=-1)
    mapped = jnp.where(usable_pick, mapped, slot)
    lead = jnp.broadcast_to(slot, mine.shape[:2] + (1,))
    picks = jnp.concatenate([lead, mapped], axis=-1)
    kinds = picks.shape[-1]
    usable = jnp.concatenate([jnp.ones(mine.shape[:2] + (1,), bool), usable_pick], axis=-1)
    sink_mine = lax.dynamic_slice_in_dim(sink, position * hpd, hpd)
    paired = jnp.concatenate(
        [
            key.reshape(seqs, unit, parts_per, hpd, width),
            value.reshape(seqs, unit, parts_per, hpd, width),
        ],
        axis=-1,
    )
    paired = jnp.transpose(paired, (2, 0, 3, 1, 4))
    items = seqs * hpd
    frag = unit * 2 * width // n_ctx
    seq_ix = jnp.arange(seqs, dtype=jnp.int32)[None, :, None, None, None]
    head_ix = jnp.arange(hpd, dtype=jnp.int32)[None, None, :, None, None]
    spread = jnp.transpose(paired.reshape(parts_per, seqs, hpd, n_ctx, frag), (3, 0, 1, 2, 4))
    held = lax.all_to_all(spread, "ctx", split_axis=0, concat_axis=0, tiled=True)
    held = jnp.transpose(held, (2, 3, 0, 1, 4)).reshape(seqs, hpd, n_ctx * parts_per, frag)
    match_block = placed[:, None] == slots[None, :]
    chosen_all = jnp.sum(jnp.where(match_block[None, :, :, None, None], chosen[:, None], 0), axis=2)
    before = chosen_all < placed[None, :, None, None]
    mapped_all = jnp.sum(jnp.where(chosen_all[..., None] == slots, slot_of, 0), axis=-1)
    own_slot = slots[None, :, None, None]
    mapped_all = jnp.where(before, mapped_all, own_slot)
    lead_all = jnp.broadcast_to(own_slot, mapped_all.shape[:3] + (1,))
    picks_all = jnp.concatenate([lead_all, mapped_all], axis=-1)
    picks_all = jnp.transpose(
        picks_all.reshape(seqs, nblk, parts_per, hpd, kinds), (1, 2, 0, 3, 4)
    ).reshape(n_ctx, seqs, hpd, kinds)
    dest_group = (jnp.arange(n_ctx, dtype=jnp.int32) % parts_per)[:, None, None, None, None]
    part_ids = jnp.arange(parts_per, dtype=jnp.int32)[None, None, None, None, :]
    route = (picks_all[..., None] * parts_per + part_ids) * parts_per + dest_group
    outgoing = held[seq_ix, head_ix, route]
    fetched = lax.all_to_all(outgoing, "ctx", split_axis=0, concat_axis=0, tiled=True)
    tiles_items = jnp.transpose(fetched, (1, 2, 3, 4, 0, 5)).reshape(
        items, kinds, parts_per * unit, 2 * width
    )
    query_heads = jnp.transpose(query.reshape(seqs, block, hpd, width), (0, 2, 1, 3)).reshape(
        items, block, width
    )
    grad_heads = jnp.transpose(grad_out.reshape(seqs, block, hpd, width), (0, 2, 1, 3)).reshape(
        items, block, width
    )
    sink_items = jnp.tile(sink_mine, seqs)

    def per_head(item):
        q_rows, g_rows, tiles, use_row, sink_logit = item
        return attend_block(q_rows, g_rows, tiles, use_row, sink_logit)

    atts, grads_q, tiles_grad, sink_grads = lax.map(
        per_head, (query_heads, grad_heads, tiles_items, usable.reshape(items, -1), sink_items)
    )
    attended = jnp.transpose(atts.reshape(seqs, hpd, block, width), (0, 2, 1, 3)).reshape(
        seqs, 1, 1, block, hpd * width
    )
    grad_query = jnp.transpose(grads_q.reshape(seqs, hpd, block, width), (0, 2, 1, 3)).reshape(
        seqs, 1, 1, block, hpd * width
    )
    shards = tiles_grad.reshape(seqs, hpd, kinds, parts_per, n_ctx, frag)
    sendback = jnp.transpose(shards, (4, 0, 1, 2, 3, 5))
    landed = lax.all_to_all(sendback, "ctx", split_axis=0, concat_axis=0, tiled=True)
    pooled = (
        jnp.zeros((seqs, hpd, n_ctx * parts_per, frag), jnp.float32)
        .at[seq_ix, head_ix, route]
        .add(landed.astype(jnp.float32))
    )
    pooled = jnp.transpose(pooled.reshape(seqs, hpd, n_ctx, parts_per, frag), (2, 3, 0, 1, 4))
    homed = lax.all_to_all(
        pooled.astype(jnp.bfloat16), "ctx", split_axis=0, concat_axis=0, tiled=True
    ).astype(pooled.dtype)
    totals = jnp.transpose(homed, (1, 2, 3, 0, 4)).reshape(parts_per, seqs, hpd, unit, 2 * width)
    totals = jnp.transpose(totals, (1, 3, 0, 2, 4))
    grad_key = totals[..., :width].reshape(seqs, unit, parts_per * hpd * width).astype(jnp.bfloat16)
    grad_value = (
        totals[..., width:].reshape(seqs, unit, parts_per * hpd * width).astype(jnp.bfloat16)
    )
    sink_local = jnp.sum(sink_grads.reshape(seqs, hpd), axis=0)
    start = lax.axis_index("head") * (parts_per * hpd) + position * hpd
    spread_sink = lax.dynamic_update_slice(jnp.zeros((HEADS,), jnp.float32), sink_local, (start,))
    grad_sink = lax.psum(spread_sink, ("dp", "ctx", "head"))
    return (attended, grad_query, grad_key, grad_value, grad_sink)


MESH = pl.DeviceIdType.MESH
ROWS = 256
LOG2E = 1.4426950408889634


def two_block_kernel(
    first, parts, hpd, unit,
    q_ref, g_ref, k_ref, v_ref, chosen_ref, sink_ref,
    att_ref, gq_ref, gk_ref, gv_ref, gs_ref,
    keys, vals, key_part, val_part, key_home, val_home, key_sum, val_sum,
    sink_part, sink_ctx, sink_peer,
    in_send, in_recv, out_send, out_recv, sink_send, sink_recv, peer_send, peer_recv,
):
    width = DH
    block = parts * unit
    scale = 1.0 / math.sqrt(width)
    me = lax.axis_index("ctx")
    slot = me // parts
    pos = me % parts
    other = 1 - slot
    is_first = slot == first
    n_ctx = 2 * parts
    mates = [slot * parts + (pos + d) % parts for d in range(1, parts)]
    across = [other * parts + (pos + d) % parts for d in range(parts)]
    peers = [ax for ax in ("head", "dp") if lax.axis_size(ax) > 1]

    barrier = pltpu.get_barrier_semaphore()
    for target in mates + across:
        pl.semaphore_signal(barrier, inc=1, device_id={"ctx": target}, device_id_type=MESH)
    for ax in peers:
        pl.semaphore_signal(barrier, inc=1, device_id={ax: 1 - lax.axis_index(ax)}, device_id_type=MESH)
    pl.semaphore_wait(barrier, n_ctx - 1 + len(peers))

    def cols(at):
        return pl.ds(pl.multiple_of(at * width, width), width)

    def fetch(h, target, source, which):
        src = (k_ref, v_ref)[which]
        dst = (keys, vals)[which]
        return pltpu.make_async_remote_copy(
            src_ref=src.at[:, cols((target % parts) * hpd + h)],
            dst_ref=dst.at[h, source],
            send_sem=in_send.at[which, h, target],
            recv_sem=in_recv.at[which, h, source],
            device_id={"ctx": target},
            device_id_type=MESH,
        )

    def give(h, target, source, which):
        src = (key_part, val_part)[which]
        dst = (key_home, val_home)[which]
        return pltpu.make_async_remote_copy(
            src_ref=src.at[h, target],
            dst_ref=dst.at[h, source],
            send_sem=out_send.at[which, h, target],
            recv_sem=out_recv.at[which, h, source],
            device_id={"ctx": target},
            device_id_type=MESH,
        )

    def each(h, targets, make, act):
        for target in targets:
            for which in range(2):
                if act == "start":
                    make(h, target, me, which).start()
                elif act == "sent":
                    make(h, target, me, which).wait_send()
                else:
                    make(h, me, target, which).wait_recv()

    half = parts // 2
    pieces = 2 * half
    ahead = pieces - 1

    def piece(h, s):
        visit, which = half - 1 - s // 2, s % 2
        targets = [other * parts + visit * 2 + t for t in range(2)]
        return [fetch(h, target, me, which) for target in targets]

    @pl.when(is_first)
    def _():
        for s in range(ahead):
            for copy in piece(0, s):
                copy.start()

    def send_head(h, carry):
        each(h, mates, fetch, "start")
        keys[h, me] = k_ref[:, cols(pos * hpd + h)]
        vals[h, me] = v_ref[:, cols(pos * hpd + h)]
        return carry

    lax.fori_loop(0, hpd, send_head, 0)

    lane = lax.broadcasted_iota(jnp.int32, (8, width), 1)
    top_row = lax.broadcasted_iota(jnp.int32, (8, width), 0) == 0
    sink_part[...] = jnp.zeros((8, width), jnp.float32)

    def share(target, source):
        return pltpu.make_async_remote_copy(
            src_ref=sink_part,
            dst_ref=sink_ctx.at[source],
            send_sem=sink_send.at[target],
            recv_sem=sink_recv.at[source],
            device_id={"ctx": target},
            device_id_type=MESH,
        )

    def keep_part(h, kind, place):
        at = pl.ds(place * parts, parts)
        key_part[h, at] = (key_sum[kind] * scale).astype(jnp.bfloat16).reshape(parts, unit, width)
        val_part[h, at] = val_sum[kind].astype(jnp.bfloat16).reshape(parts, unit, width)

    def back(kind, r, n, q, g, k, v, p, w, delta):
        ds = (p * (inner_rows(g, v) - delta)).astype(jnp.bfloat16)
        dk = outer_rows(ds, q)
        dv = outer_rows(w, g)
        if r == 0:
            key_sum[kind, :n] = dk
            val_sum[kind, :n] = dv
            if n < block:
                key_sum[kind, n:] = jnp.zeros((block - n, width), jnp.float32)
                val_sum[kind, n:] = jnp.zeros((block - n, width), jnp.float32)
        else:
            key_sum[kind, :n] += dk
            val_sum[kind, :n] += dv
        return jnp.dot(ds, k, preferred_element_type=jnp.float32)

    def attend(h, with_other):
        local_head = pos * hpd + h
        k_own = keys[h, pl.ds(slot * parts, parts)].reshape(block, width)
        v_own = vals[h, pl.ds(slot * parts, parts)].reshape(block, width)
        sink_logit = sink_ref[local_head] * LOG2E
        if with_other:
            k_oth = keys[h, pl.ds(other * parts, parts)].reshape(block, width)
            v_oth = vals[h, pl.ds(other * parts, parts)].reshape(block, width)
            sees = chosen_ref[0, 1, local_head, 0] < 1
            for entry in range(1, chosen_ref.shape[3]):
                sees = jnp.logical_or(sees, chosen_ref[0, 1, local_head, entry] < 1)
        sink_total = jnp.zeros((1, 1), jnp.float32)
        kept = []
        for r in range(block // ROWS):
            rows = pl.ds(r * ROWS, ROWS)
            q = q_ref[rows, cols(h)]
            g = g_ref[rows, cols(h)]
            n = (r + 1) * ROWS
            k, v = k_own[:n], v_own[:n]
            s = inner_rows(q, k) * (scale * LOG2E)
            at_row = lax.broadcasted_iota(jnp.int32, (ROWS, n), 0) + r * ROWS
            at_col = lax.broadcasted_iota(jnp.int32, (ROWS, n), 1)
            s = jnp.where(at_col <= at_row, s, -jnp.inf)
            top = jnp.maximum(jnp.max(s, axis=1, keepdims=True), sink_logit)
            if with_other:
                s_oth = inner_rows(q, k_oth) * (scale * LOG2E)
                top_oth = jnp.max(s_oth, axis=1, keepdims=True)
                top = jnp.maximum(top, jnp.where(sees, top_oth, -jnp.inf))
                e_oth = jnp.exp2(s_oth - jnp.where(sees, top, jnp.inf))
            e = jnp.exp2(s - top)
            sink_exp = jnp.exp2(sink_logit - top)
            total = sink_exp + jnp.sum(e, axis=1, keepdims=True)
            if with_other:
                total = total + jnp.sum(e_oth, axis=1, keepdims=True)
            inv = 1.0 / total
            p = e * inv
            w = p.astype(jnp.bfloat16)
            out = jnp.dot(w, v, preferred_element_type=jnp.float32)
            if with_other:
                p_oth = e_oth * inv
                w_oth = p_oth.astype(jnp.bfloat16)
                out = out + jnp.dot(w_oth, v_oth, preferred_element_type=jnp.float32)
            out = out.astype(jnp.bfloat16)
            att_ref[rows, cols(h)] = out
            delta = jnp.sum(g.astype(jnp.float32) * out.astype(jnp.float32), axis=1, keepdims=True)
            sink_total = sink_total - jnp.sum(sink_exp * inv * delta, axis=0, keepdims=True)
            gq = jnp.zeros((ROWS, width), jnp.float32)
            if with_other:
                gq = back(1, r, block, q, g, k_oth, v_oth, p_oth, w_oth, delta)
            kept.append((r, n, q, g, k, v, p, w, delta, gq))
        mine = jnp.logical_and(lane == lax.axis_index("head") * (parts * hpd) + local_head, top_row)
        sink_part[...] += jnp.where(mine, sink_total, 0.0)

        @pl.when(h == hpd - 1)
        def _():
            for target in mates + across:
                share(target, me).start()
        if with_other:
            keep_part(h, 1, other)
            each(h, across, give, "start")
        for r, n, q, g, k, v, p, w, delta, gq in kept:
            gq = gq + back(0, r, n, q, g, k, v, p, w, delta)
            gq_ref[pl.ds(r * ROWS, ROWS), cols(h)] = (gq * scale).astype(jnp.bfloat16)
        keep_part(h, 0, slot)

    def head_step(h, carry):
        @pl.when(is_first)
        def _():
            for gone, late in zip(piece(h, 0), piece(h, ahead)):
                gone.wait_send()
                late.start()

        @pl.when(jnp.logical_and(is_first, h < hpd - 1))
        def _():
            for s in range(1, pieces):
                for gone, late in zip(piece(h, s), piece(h + 1, s - 1)):
                    gone.wait_send()
                    late.start()

        each(h, mates, fetch, "arrived")

        @pl.when(is_first)
        def _():
            attend(h, False)

        @pl.when(jnp.logical_not(is_first))
        def _():
            each(h, across, fetch, "arrived")
            attend(h, True)

        each(h, mates, give, "start")
        key_home[h, me] = key_part[h, me]
        val_home[h, me] = val_part[h, me]
        return carry

    lax.fori_loop(0, hpd, head_step, 0)

    sink_ctx[me] = sink_part[...]
    for target in mates + across:
        share(me, target).wait_recv()
    gathered = sink_ctx[0]
    for source in range(1, n_ctx):
        gathered = gathered + sink_ctx[source]
    for at, ax in enumerate(peers):
        sink_peer[2 * at] = gathered
        swap = pltpu.make_async_remote_copy(
            src_ref=sink_peer.at[2 * at],
            dst_ref=sink_peer.at[2 * at + 1],
            send_sem=peer_send.at[at],
            recv_sem=peer_recv.at[at],
            device_id={ax: 1 - lax.axis_index(ax)},
            device_id_type=MESH,
        )
        swap.start()
        swap.wait()
        gathered = gathered + sink_peer[2 * at + 1]
    gs_ref[...] = gathered

    def finish(h, carry):
        each(h, mates, give, "arrived")

        @pl.when(is_first)
        def _():
            each(h, across, give, "arrived")
            for p in range(parts):
                for home, out in ((key_home, gk_ref), (val_home, gv_ref)):
                    a = home[h, slot * parts + p].astype(jnp.float32)
                    b = home[h, other * parts + p].astype(jnp.float32)
                    out[:, cols(p * hpd + h)] = (a + b).astype(jnp.bfloat16)

        @pl.when(jnp.logical_not(is_first))
        def _():
            for p in range(parts):
                for home, out in ((key_home, gk_ref), (val_home, gv_ref)):
                    out[:, cols(p * hpd + h)] = home[h, slot * parts + p]
        return carry

    lax.fori_loop(0, hpd, finish, 0)

    def drain(h, carry):
        @pl.when(jnp.logical_and(is_first, h == hpd - 1))
        def _():
            for s in range(1, pieces):
                for copy in piece(h, s):
                    copy.wait_send()

        @pl.when(jnp.logical_not(is_first))
        def _():
            each(h, across, give, "sent")
        each(h, mates, fetch, "sent")
        each(h, mates, give, "sent")
        return carry

    lax.fori_loop(0, hpd, drain, 0)
    for target in mates + across:
        share(target, me).wait_send()


def two_block_call(first, parts, hpd, q, g, k, v, chosen, sink):
    unit = k.shape[0]
    block = parts * unit
    n_ctx = 2 * parts
    vmem = pl.BlockSpec(memory_space=pltpu.VMEM)
    smem = pl.BlockSpec(memory_space=pltpu.SMEM)
    slots = pltpu.VMEM((hpd, n_ctx, unit, DH), jnp.bfloat16)
    sums = pltpu.VMEM((2, block, DH), jnp.float32)
    dma = pltpu.SemaphoreType.DMA
    bf16 = jnp.bfloat16
    return pl.pallas_call(
        functools.partial(two_block_kernel, first, parts, hpd, unit),
        out_shape=(
            jax.ShapeDtypeStruct(q.shape, bf16),
            jax.ShapeDtypeStruct(q.shape, bf16),
            jax.ShapeDtypeStruct(k.shape, bf16),
            jax.ShapeDtypeStruct(k.shape, bf16),
            jax.ShapeDtypeStruct((8, DH), jnp.float32),
        ),
        in_specs=[vmem, vmem, vmem, vmem, smem, smem],
        out_specs=(vmem,) * 5,
        scratch_shapes=[
            slots, slots, slots, slots, slots, slots, sums, sums,
            pltpu.VMEM((8, DH), jnp.float32),
            pltpu.VMEM((n_ctx, 8, DH), jnp.float32),
            pltpu.VMEM((4, 8, DH), jnp.float32),
            dma((2, hpd, n_ctx)), dma((2, hpd, n_ctx)),
            dma((2, hpd, n_ctx)), dma((2, hpd, n_ctx)),
            dma((n_ctx,)), dma((n_ctx,)), dma((2,)), dma((2,)),
        ],
        compiler_params=pltpu.CompilerParams(
            collective_id=first, has_side_effects=True, vmem_limit_bytes=40 * 1024 * 1024
        ),
        name=f"two_block_{first}",
    )(q, g, k, v, chosen, sink)


def put_kernel(n, *refs):
    sems = refs[-1]
    copies = [pltpu.make_async_copy(refs[i], refs[n + i], sems.at[i]) for i in range(n)]
    for copy in copies:
        copy.start()
    for copy in copies:
        copy.wait()


def put_results(*arrays):
    n = len(arrays)
    anywhere = pl.BlockSpec(memory_space=pl.ANY)
    return pl.pallas_call(
        functools.partial(put_kernel, n),
        out_shape=tuple(jax.ShapeDtypeStruct(a.shape, a.dtype) for a in arrays),
        in_specs=[anywhere] * n,
        out_specs=(anywhere,) * n,
        scratch_shapes=[pltpu.SemaphoreType.DMA((n,))],
        name="put_results",
    )(*arrays)


def two_block_body(query, key, value, grad_out, chosen, placed, sink):
    block = query.shape[3]
    unit = key.shape[1]
    parts = block // unit
    hpd = query.shape[4] // DH
    q = query.reshape(block, hpd * DH)
    g = grad_out.reshape(block, hpd * DH)
    k = key.reshape(unit, -1)
    v = value.reshape(unit, -1)
    att, gq, gk, gv, gs = lax.cond(
        placed[0] == 0,
        functools.partial(two_block_call, 0, parts, hpd),
        functools.partial(two_block_call, 1, parts, hpd),
        q, g, k, v, chosen, sink,
    )
    att, gq, gk, gv = put_results(att, gq, gk, gv)
    return (
        att.reshape(query.shape),
        gq.reshape(query.shape),
        gk.reshape(key.shape),
        gv.reshape(key.shape),
        gs[0, :HEADS],
    )


def body(query, key, value, grad_out, chosen, placed, sink):
    parts = query.shape[3] // key.shape[1]
    if query.shape[0] == 1 and lax.axis_size("ctx") == 2 * parts:
        return two_block_body(query, key, value, grad_out, chosen, placed, sink)
    return general_body(query, key, value, grad_out, chosen, placed, sink)


def solution(mesh):
    in_specs = (
        P("dp", "ctx", "head", None, None),
        P("dp", "ctx", "head"),
        P("dp", "ctx", "head"),
        P("dp", "ctx", "head", None, None),
        P("dp", None, "head", None),
        P(),
        P("head"),
    )
    out_specs = (
        P("dp", "ctx", "head", None, None),
        P("dp", "ctx", "head", None, None),
        P("dp", "ctx", "head"),
        P("dp", "ctx", "head"),
        P(),
    )
    return jax.shard_map(body, mesh=mesh, in_specs=in_specs, out_specs=out_specs, check_vma=False)
```

```python
import functools
import math

import jax
import jax.numpy as jnp
from jax import lax
from jax.experimental import pallas as pl
from jax.experimental.pallas import tpu as pltpu
from jax.sharding import PartitionSpec as P

HEADS = 32
DH = 128


def inner_rows(left, right):
    return lax.dot_general(
        left, right, (((1,), (1,)), ((), ())), preferred_element_type=jnp.float32
    )


def outer_rows(left, right):
    return lax.dot_general(
        left, right, (((0,), (0,)), ((), ())), preferred_element_type=jnp.float32
    )


def attend_block(query_rows, grad_rows, tiles, usable, sink_logit):
    rows, width = query_rows.shape
    scale = 1.0 / math.sqrt(width)
    keys = tiles[:, :, :width].reshape(-1, width)
    vals = tiles[:, :, width:].reshape(-1, width)
    scores = inner_rows(query_rows, keys) * scale
    cols = tiles.shape[0] * rows
    tile_of = jnp.arange(cols) // rows
    offset = jnp.arange(cols) % rows
    own_ok = offset[None, :] <= jnp.arange(rows)[:, None]
    allowed = jnp.where(tile_of[None, :] == 0, own_ok, usable[tile_of][None, :])
    masked = jnp.where(allowed, scores, -jnp.inf)
    top = jnp.maximum(jnp.max(masked, axis=1), sink_logit)
    expo = jnp.exp(masked - top[:, None])
    sink_part = jnp.exp(sink_logit - top)
    total = sink_part + jnp.sum(expo, axis=1)
    prob = expo / total[:, None]
    weights = prob.astype(jnp.bfloat16)
    attended = jnp.dot(weights, vals, preferred_element_type=jnp.float32).astype(jnp.bfloat16)
    stored = lax.optimization_barrier(attended)
    delta = jnp.sum(grad_rows.astype(jnp.float32) * stored.astype(jnp.float32), axis=1)
    dprob = inner_rows(grad_rows, vals)
    dscore = (prob * (dprob - delta[:, None]) * scale).astype(jnp.bfloat16)
    grad_query = jnp.dot(dscore, keys, preferred_element_type=jnp.float32).astype(jnp.bfloat16)
    grad_keys = outer_rows(dscore, query_rows).astype(jnp.bfloat16)
    grad_vals = outer_rows(weights, grad_rows).astype(jnp.bfloat16)
    tiles_grad = jnp.concatenate([grad_keys, grad_vals], axis=1).reshape(tiles.shape)
    sink_grad = -jnp.sum(sink_part / total * delta)
    return (attended, grad_query, tiles_grad, sink_grad)


def general_body(query, key, value, grad_out, chosen, placed, sink):
    seqs = query.shape[0]
    block = query.shape[3]
    width = DH
    hpd = query.shape[4] // width
    unit = key.shape[1]
    parts_per = block // unit
    n_ctx = lax.axis_size("ctx")
    nblk = n_ctx // parts_per
    place = lax.axis_index("ctx")
    slot = place // parts_per
    position = place % parts_per
    slots = jnp.arange(nblk, dtype=jnp.int32)
    seq_block = jnp.sum(jnp.where(slots == slot, placed, 0))
    slot_of = jnp.sum(jnp.where(placed[None, :] == slots[:, None], slots[None, :], 0), axis=1)
    mine = lax.dynamic_slice_in_dim(chosen, seq_block, 1, 1)[:, 0]
    mine = lax.dynamic_slice_in_dim(mine, position * hpd, hpd, 1)
    usable_pick = mine < seq_block
    mapped = jnp.sum(jnp.where(mine[..., None] == slots, slot_of, 0), axis=-1)
    mapped = jnp.where(usable_pick, mapped, slot)
    lead = jnp.broadcast_to(slot, mine.shape[:2] + (1,))
    picks = jnp.concatenate([lead, mapped], axis=-1)
    kinds = picks.shape[-1]
    usable = jnp.concatenate([jnp.ones(mine.shape[:2] + (1,), bool), usable_pick], axis=-1)
    sink_mine = lax.dynamic_slice_in_dim(sink, position * hpd, hpd)
    paired = jnp.concatenate(
        [
            key.reshape(seqs, unit, parts_per, hpd, width),
            value.reshape(seqs, unit, parts_per, hpd, width),
        ],
        axis=-1,
    )
    paired = jnp.transpose(paired, (2, 0, 3, 1, 4))
    items = seqs * hpd
    frag = unit * 2 * width // n_ctx
    seq_ix = jnp.arange(seqs, dtype=jnp.int32)[None, :, None, None, None]
    head_ix = jnp.arange(hpd, dtype=jnp.int32)[None, None, :, None, None]
    spread = jnp.transpose(paired.reshape(parts_per, seqs, hpd, n_ctx, frag), (3, 0, 1, 2, 4))
    held = lax.all_to_all(spread, "ctx", split_axis=0, concat_axis=0, tiled=True)
    held = jnp.transpose(held, (2, 3, 0, 1, 4)).reshape(seqs, hpd, n_ctx * parts_per, frag)
    match_block = placed[:, None] == slots[None, :]
    chosen_all = jnp.sum(jnp.where(match_block[None, :, :, None, None], chosen[:, None], 0), axis=2)
    before = chosen_all < placed[None, :, None, None]
    mapped_all = jnp.sum(jnp.where(chosen_all[..., None] == slots, slot_of, 0), axis=-1)
    own_slot = slots[None, :, None, None]
    mapped_all = jnp.where(before, mapped_all, own_slot)
    lead_all = jnp.broadcast_to(own_slot, mapped_all.shape[:3] + (1,))
    picks_all = jnp.concatenate([lead_all, mapped_all], axis=-1)
    picks_all = jnp.transpose(
        picks_all.reshape(seqs, nblk, parts_per, hpd, kinds), (1, 2, 0, 3, 4)
    ).reshape(n_ctx, seqs, hpd, kinds)
    dest_group = (jnp.arange(n_ctx, dtype=jnp.int32) % parts_per)[:, None, None, None, None]
    part_ids = jnp.arange(parts_per, dtype=jnp.int32)[None, None, None, None, :]
    route = (picks_all[..., None] * parts_per + part_ids) * parts_per + dest_group
    outgoing = held[seq_ix, head_ix, route]
    fetched = lax.all_to_all(outgoing, "ctx", split_axis=0, concat_axis=0, tiled=True)
    tiles_items = jnp.transpose(fetched, (1, 2, 3, 4, 0, 5)).reshape(
        items, kinds, parts_per * unit, 2 * width
    )
    query_heads = jnp.transpose(query.reshape(seqs, block, hpd, width), (0, 2, 1, 3)).reshape(
        items, block, width
    )
    grad_heads = jnp.transpose(grad_out.reshape(seqs, block, hpd, width), (0, 2, 1, 3)).reshape(
        items, block, width
    )
    sink_items = jnp.tile(sink_mine, seqs)

    def per_head(item):
        q_rows, g_rows, tiles, use_row, sink_logit = item
        return attend_block(q_rows, g_rows, tiles, use_row, sink_logit)

    atts, grads_q, tiles_grad, sink_grads = lax.map(
        per_head, (query_heads, grad_heads, tiles_items, usable.reshape(items, -1), sink_items)
    )
    attended = jnp.transpose(atts.reshape(seqs, hpd, block, width), (0, 2, 1, 3)).reshape(
        seqs, 1, 1, block, hpd * width
    )
    grad_query = jnp.transpose(grads_q.reshape(seqs, hpd, block, width), (0, 2, 1, 3)).reshape(
        seqs, 1, 1, block, hpd * width
    )
    shards = tiles_grad.reshape(seqs, hpd, kinds, parts_per, n_ctx, frag)
    sendback = jnp.transpose(shards, (4, 0, 1, 2, 3, 5))
    landed = lax.all_to_all(sendback, "ctx", split_axis=0, concat_axis=0, tiled=True)
    pooled = (
        jnp.zeros((seqs, hpd, n_ctx * parts_per, frag), jnp.float32)
        .at[seq_ix, head_ix, route]
        .add(landed.astype(jnp.float32))
    )
    pooled = jnp.transpose(pooled.reshape(seqs, hpd, n_ctx, parts_per, frag), (2, 3, 0, 1, 4))
    homed = lax.all_to_all(
        pooled.astype(jnp.bfloat16), "ctx", split_axis=0, concat_axis=0, tiled=True
    ).astype(pooled.dtype)
    totals = jnp.transpose(homed, (1, 2, 3, 0, 4)).reshape(parts_per, seqs, hpd, unit, 2 * width)
    totals = jnp.transpose(totals, (1, 3, 0, 2, 4))
    grad_key = totals[..., :width].reshape(seqs, unit, parts_per * hpd * width).astype(jnp.bfloat16)
    grad_value = (
        totals[..., width:].reshape(seqs, unit, parts_per * hpd * width).astype(jnp.bfloat16)
    )
    sink_local = jnp.sum(sink_grads.reshape(seqs, hpd), axis=0)
    start = lax.axis_index("head") * (parts_per * hpd) + position * hpd
    spread_sink = lax.dynamic_update_slice(jnp.zeros((HEADS,), jnp.float32), sink_local, (start,))
    grad_sink = lax.psum(spread_sink, ("dp", "ctx", "head"))
    return (attended, grad_query, grad_key, grad_value, grad_sink)


MESH = pl.DeviceIdType.MESH
ROWS = 256
LOG2E = 1.4426950408889634


def two_block_kernel(
    first, parts, hpd, unit,
    q_ref, g_ref, k_ref, v_ref, chosen_ref, sink_ref,
    att_ref, gq_ref, gk_ref, gv_ref, gs_ref,
    keys, vals, key_part, val_part, key_home, val_home, key_sum, val_sum,
    sink_part, sink_ctx, sink_peer,
    in_send, in_recv, out_send, out_recv, sink_send, sink_recv, peer_send, peer_recv,
):
    width = DH
    block = parts * unit
    scale = 1.0 / math.sqrt(width)
    me = lax.axis_index("ctx")
    slot = me // parts
    pos = me % parts
    other = 1 - slot
    is_first = slot == first
    n_ctx = 2 * parts
    mates = [slot * parts + (pos + d) % parts for d in range(1, parts)]
    across = [other * parts + (pos + d) % parts for d in range(parts)]
    peers = [ax for ax in ("head", "dp") if lax.axis_size(ax) > 1]

    barrier = pltpu.get_barrier_semaphore()
    for target in mates + across:
        pl.semaphore_signal(barrier, inc=1, device_id={"ctx": target}, device_id_type=MESH)
    for ax in peers:
        pl.semaphore_signal(barrier, inc=1, device_id={ax: 1 - lax.axis_index(ax)}, device_id_type=MESH)
    pl.semaphore_wait(barrier, n_ctx - 1 + len(peers))

    def cols(at):
        return pl.ds(pl.multiple_of(at * width, width), width)

    def fetch(h, target, source, which):
        src = (k_ref, v_ref)[which]
        dst = (keys, vals)[which]
        return pltpu.make_async_remote_copy(
            src_ref=src.at[:, cols((target % parts) * hpd + h)],
            dst_ref=dst.at[h, source],
            send_sem=in_send.at[which, h, target],
            recv_sem=in_recv.at[which, h, source],
            device_id={"ctx": target},
            device_id_type=MESH,
        )

    def give(h, target, source, which):
        src = (key_part, val_part)[which]
        dst = (key_home, val_home)[which]
        return pltpu.make_async_remote_copy(
            src_ref=src.at[h, target],
            dst_ref=dst.at[h, source],
            send_sem=out_send.at[which, h, target],
            recv_sem=out_recv.at[which, h, source],
            device_id={"ctx": target},
            device_id_type=MESH,
        )

    def each(h, targets, make, act):
        for target in targets:
            for which in range(2):
                if act == "start":
                    make(h, target, me, which).start()
                elif act == "sent":
                    make(h, target, me, which).wait_send()
                else:
                    make(h, me, target, which).wait_recv()

    half = parts // 2
    pieces = 2 * half
    ahead = pieces - 1

    def piece(h, s):
        visit, which = s // 2, s % 2
        if first == 0:
            visit = half - 1 - visit
        targets = [other * parts + visit * 2 + t for t in range(2)]
        return [fetch(h, target, me, which) for target in targets]

    @pl.when(is_first)
    def _():
        for s in range(ahead):
            for copy in piece(0, s):
                copy.start()

    def send_head(h, carry):
        @pl.when(jnp.logical_or(jnp.logical_not(is_first), h == 0))
        def _():
            each(h, mates, fetch, "start")

        keys[h, me] = k_ref[:, cols(pos * hpd + h)]
        vals[h, me] = v_ref[:, cols(pos * hpd + h)]
        return carry

    lax.fori_loop(0, hpd, send_head, 0)

    lane = lax.broadcasted_iota(jnp.int32, (8, width), 1)
    top_row = lax.broadcasted_iota(jnp.int32, (8, width), 0) == 0
    sink_part[...] = jnp.zeros((8, width), jnp.float32)

    def share(target, source):
        return pltpu.make_async_remote_copy(
            src_ref=sink_part,
            dst_ref=sink_ctx.at[source],
            send_sem=sink_send.at[target],
            recv_sem=sink_recv.at[source],
            device_id={"ctx": target},
            device_id_type=MESH,
        )

    def keep_part(h, kind, place):
        at = pl.ds(place * parts, parts)
        key_part[h, at] = (key_sum[kind] * scale).astype(jnp.bfloat16).reshape(parts, unit, width)
        val_part[h, at] = val_sum[kind].astype(jnp.bfloat16).reshape(parts, unit, width)

    def back(kind, r, n, q, g, k, v, p, w, delta):
        ds = (p * (inner_rows(g, v) - delta)).astype(jnp.bfloat16)
        dk = outer_rows(ds, q)
        dv = outer_rows(w, g)
        if r == 0:
            key_sum[kind, :n] = dk
            val_sum[kind, :n] = dv
            if n < block:
                key_sum[kind, n:] = jnp.zeros((block - n, width), jnp.float32)
                val_sum[kind, n:] = jnp.zeros((block - n, width), jnp.float32)
        else:
            key_sum[kind, :n] += dk
            val_sum[kind, :n] += dv
        return jnp.dot(ds, k, preferred_element_type=jnp.float32)

    def attend(h, with_other):
        local_head = pos * hpd + h
        k_own = keys[h, pl.ds(slot * parts, parts)].reshape(block, width)
        v_own = vals[h, pl.ds(slot * parts, parts)].reshape(block, width)
        sink_logit = sink_ref[local_head] * LOG2E
        if with_other:
            k_oth = keys[h, pl.ds(other * parts, parts)].reshape(block, width)
            v_oth = vals[h, pl.ds(other * parts, parts)].reshape(block, width)
            sees = chosen_ref[0, 1, local_head, 0] < 1
            for entry in range(1, chosen_ref.shape[3]):
                sees = jnp.logical_or(sees, chosen_ref[0, 1, local_head, entry] < 1)
        sink_total = jnp.zeros((1, 1), jnp.float32)
        kept = []
        for r in range(block // ROWS):
            rows = pl.ds(r * ROWS, ROWS)
            q = q_ref[rows, cols(h)]
            g = g_ref[rows, cols(h)]
            n = (r + 1) * ROWS
            k, v = k_own[:n], v_own[:n]
            s = inner_rows(q, k) * (scale * LOG2E)
            at_row = lax.broadcasted_iota(jnp.int32, (ROWS, n), 0) + r * ROWS
            at_col = lax.broadcasted_iota(jnp.int32, (ROWS, n), 1)
            s = jnp.where(at_col <= at_row, s, -jnp.inf)
            top = jnp.maximum(jnp.max(s, axis=1, keepdims=True), sink_logit)
            if with_other:
                s_oth = inner_rows(q, k_oth) * (scale * LOG2E)
                top_oth = jnp.max(s_oth, axis=1, keepdims=True)
                top = jnp.maximum(top, jnp.where(sees, top_oth, -jnp.inf))
                e_oth = jnp.exp2(s_oth - jnp.where(sees, top, jnp.inf))
            e = jnp.exp2(s - top)
            sink_exp = jnp.exp2(sink_logit - top)
            total = sink_exp + jnp.sum(e, axis=1, keepdims=True)
            if with_other:
                total = total + jnp.sum(e_oth, axis=1, keepdims=True)
            inv = 1.0 / total
            p = e * inv
            w = p.astype(jnp.bfloat16)
            out = jnp.dot(w, v, preferred_element_type=jnp.float32)
            if with_other:
                p_oth = e_oth * inv
                w_oth = p_oth.astype(jnp.bfloat16)
                out = out + jnp.dot(w_oth, v_oth, preferred_element_type=jnp.float32)
            out = out.astype(jnp.bfloat16)
            att_ref[rows, cols(h)] = out
            delta = jnp.sum(g.astype(jnp.float32) * out.astype(jnp.float32), axis=1, keepdims=True)
            sink_total = sink_total - jnp.sum(sink_exp * inv * delta, axis=0, keepdims=True)
            gq = jnp.zeros((ROWS, width), jnp.float32)
            if with_other:
                gq = back(1, r, block, q, g, k_oth, v_oth, p_oth, w_oth, delta)
            kept.append((r, n, q, g, k, v, p, w, delta, gq))
        mine = jnp.logical_and(lane == lax.axis_index("head") * (parts * hpd) + local_head, top_row)
        sink_part[...] += jnp.where(mine, sink_total, 0.0)

        @pl.when(h == hpd - 1)
        def _():
            for target in mates + across:
                share(target, me).start()
        if with_other:
            keep_part(h, 1, other)
            each(h, across, give, "start")
        for r, n, q, g, k, v, p, w, delta, gq in kept:
            gq = gq + back(0, r, n, q, g, k, v, p, w, delta)
            gq_ref[pl.ds(r * ROWS, ROWS), cols(h)] = (gq * scale).astype(jnp.bfloat16)
        keep_part(h, 0, slot)

    def head_step(h, carry):
        @pl.when(is_first)
        def _():
            for gone, late in zip(piece(h, 0), piece(h, ahead)):
                gone.wait_send()
                late.start()

        @pl.when(jnp.logical_and(is_first, h < hpd - 1))
        def _():
            each(h + 1, mates, fetch, "start")
            for s in range(1, pieces):
                for gone, late in zip(piece(h, s), piece(h + 1, s - 1)):
                    gone.wait_send()
                    late.start()

        each(h, mates, fetch, "arrived")

        @pl.when(is_first)
        def _():
            attend(h, False)

        @pl.when(jnp.logical_not(is_first))
        def _():
            each(h, across, fetch, "arrived")
            attend(h, True)

        each(h, mates, give, "start")
        key_home[h, me] = key_part[h, me]
        val_home[h, me] = val_part[h, me]
        return carry

    lax.fori_loop(0, hpd, head_step, 0)

    sink_ctx[me] = sink_part[...]
    for target in mates + across:
        share(me, target).wait_recv()
    gathered = sink_ctx[0]
    for source in range(1, n_ctx):
        gathered = gathered + sink_ctx[source]
    for at, ax in enumerate(peers):
        sink_peer[2 * at] = gathered
        swap = pltpu.make_async_remote_copy(
            src_ref=sink_peer.at[2 * at],
            dst_ref=sink_peer.at[2 * at + 1],
            send_sem=peer_send.at[at],
            recv_sem=peer_recv.at[at],
            device_id={ax: 1 - lax.axis_index(ax)},
            device_id_type=MESH,
        )
        swap.start()
        swap.wait()
        gathered = gathered + sink_peer[2 * at + 1]
    gs_ref[...] = gathered

    def finish(h, carry):
        each(h, mates, give, "arrived")

        @pl.when(is_first)
        def _():
            each(h, across, give, "arrived")
            for p in range(parts):
                for home, out in ((key_home, gk_ref), (val_home, gv_ref)):
                    a = home[h, slot * parts + p].astype(jnp.float32)
                    b = home[h, other * parts + p].astype(jnp.float32)
                    out[:, cols(p * hpd + h)] = (a + b).astype(jnp.bfloat16)

        @pl.when(jnp.logical_not(is_first))
        def _():
            for p in range(parts):
                for home, out in ((key_home, gk_ref), (val_home, gv_ref)):
                    out[:, cols(p * hpd + h)] = home[h, slot * parts + p]
        return carry

    lax.fori_loop(0, hpd, finish, 0)

    def drain(h, carry):
        @pl.when(jnp.logical_and(is_first, h == hpd - 1))
        def _():
            for s in range(1, pieces):
                for copy in piece(h, s):
                    copy.wait_send()

        @pl.when(jnp.logical_not(is_first))
        def _():
            each(h, across, give, "sent")
        each(h, mates, fetch, "sent")
        each(h, mates, give, "sent")
        return carry

    lax.fori_loop(0, hpd, drain, 0)
    for target in mates + across:
        share(target, me).wait_send()


def two_block_call(first, parts, hpd, q, g, k, v, chosen, sink):
    unit = k.shape[0]
    block = parts * unit
    n_ctx = 2 * parts
    vmem = pl.BlockSpec(memory_space=pltpu.VMEM)
    smem = pl.BlockSpec(memory_space=pltpu.SMEM)
    slots = pltpu.VMEM((hpd, n_ctx, unit, DH), jnp.bfloat16)
    sums = pltpu.VMEM((2, block, DH), jnp.float32)
    dma = pltpu.SemaphoreType.DMA
    bf16 = jnp.bfloat16
    return pl.pallas_call(
        functools.partial(two_block_kernel, first, parts, hpd, unit),
        out_shape=(
            jax.ShapeDtypeStruct(q.shape, bf16),
            jax.ShapeDtypeStruct(q.shape, bf16),
            jax.ShapeDtypeStruct(k.shape, bf16),
            jax.ShapeDtypeStruct(k.shape, bf16),
            jax.ShapeDtypeStruct((8, DH), jnp.float32),
        ),
        in_specs=[vmem, vmem, vmem, vmem, smem, smem],
        out_specs=(vmem,) * 5,
        scratch_shapes=[
            slots, slots, slots, slots, slots, slots, sums, sums,
            pltpu.VMEM((8, DH), jnp.float32),
            pltpu.VMEM((n_ctx, 8, DH), jnp.float32),
            pltpu.VMEM((4, 8, DH), jnp.float32),
            dma((2, hpd, n_ctx)), dma((2, hpd, n_ctx)),
            dma((2, hpd, n_ctx)), dma((2, hpd, n_ctx)),
            dma((n_ctx,)), dma((n_ctx,)), dma((2,)), dma((2,)),
        ],
        compiler_params=pltpu.CompilerParams(
            collective_id=first, has_side_effects=True, vmem_limit_bytes=40 * 1024 * 1024
        ),
        name=f"two_block_{first}",
    )(q, g, k, v, chosen, sink)


def put_kernel(n, *refs):
    sems = refs[-1]
    copies = [pltpu.make_async_copy(refs[i], refs[n + i], sems.at[i]) for i in range(n)]
    for copy in copies:
        copy.start()
    for copy in copies:
        copy.wait()


def put_results(*arrays):
    n = len(arrays)
    anywhere = pl.BlockSpec(memory_space=pl.ANY)
    return pl.pallas_call(
        functools.partial(put_kernel, n),
        out_shape=tuple(jax.ShapeDtypeStruct(a.shape, a.dtype) for a in arrays),
        in_specs=[anywhere] * n,
        out_specs=(anywhere,) * n,
        scratch_shapes=[pltpu.SemaphoreType.DMA((n,))],
        name="put_results",
    )(*arrays)


def two_block_body(query, key, value, grad_out, chosen, placed, sink):
    block = query.shape[3]
    unit = key.shape[1]
    parts = block // unit
    hpd = query.shape[4] // DH
    q = query.reshape(block, hpd * DH)
    g = grad_out.reshape(block, hpd * DH)
    k = key.reshape(unit, -1)
    v = value.reshape(unit, -1)
    att, gq, gk, gv, gs = lax.cond(
        placed[0] == 0,
        functools.partial(two_block_call, 0, parts, hpd),
        functools.partial(two_block_call, 1, parts, hpd),
        q, g, k, v, chosen, sink,
    )
    att, gq, gk, gv = put_results(att, gq, gk, gv)
    return (
        att.reshape(query.shape),
        gq.reshape(query.shape),
        gk.reshape(key.shape),
        gv.reshape(key.shape),
        gs[0, :HEADS],
    )


def body(query, key, value, grad_out, chosen, placed, sink):
    parts = query.shape[3] // key.shape[1]
    if query.shape[0] == 1 and lax.axis_size("ctx") == 2 * parts:
        return two_block_body(query, key, value, grad_out, chosen, placed, sink)
    return general_body(query, key, value, grad_out, chosen, placed, sink)


def solution(mesh):
    in_specs = (
        P("dp", "ctx", "head", None, None),
        P("dp", "ctx", "head"),
        P("dp", "ctx", "head"),
        P("dp", "ctx", "head", None, None),
        P("dp", None, "head", None),
        P(),
        P("head"),
    )
    out_specs = (
        P("dp", "ctx", "head", None, None),
        P("dp", "ctx", "head", None, None),
        P("dp", "ctx", "head"),
        P("dp", "ctx", "head"),
        P(),
    )
    return jax.shard_map(body, mesh=mesh, in_specs=in_specs, out_specs=out_specs, check_vma=False)
```
